32 devices in a mesh: groups: 2 (over y), seq: 4 (over z), chan: 4 (over x, core).
Axes of the slice: x: 2, y: 2, z: 4, core: 2. Of those that a mesh axis runs over, the one named last changes fastest.
Arguments:
- x_in: bfloat16 [3072, 8192], P(('groups', 'seq'), 'chan'), parts along dimension 0, may hold values from -6 to 6
- b_in: bfloat16 [3072, 8, 128], P(('groups', 'seq'), 'chan'), parts along dimension 0, may hold values from -6 to 6
- c_in: bfloat16 [3072, 8, 128], P(('groups', 'seq'), 'chan'), parts along dimension 0, may hold values from -6 to 6
- dt_in: float32 [3072, 128], P(('groups', 'seq'), 'chan'), parts along dimension 0, may hold values from -1.1 to 3.3
- a_log: float32 [128], P('chan'), may hold values from -11 to -3.4
- z_in: bfloat16 [3072, 8192], P(('groups', 'seq'), 'chan'), parts along dimension 0, may hold values from -6 to 6
- conv_x: float32 [4, 8192], P(None, 'chan'), may hold values from -3 to 3
- conv_bc: float32 [2, 4, 8, 128], P(None, None, 'chan'), may hold values from -3 to 3
- norm_gain: float32 [8192], P('chan'), may hold values from 0.25 to 1.75
- w_kv: bfloat16 [8192, 8, 256], P('chan'), may hold values from -1 to 1
- queries: bfloat16 [3072, 64, 128], P(('groups', 'seq'), 'chan'), parts along dimension 0, may hold values from -40 to 40
Outputs:
- mixer_out: bfloat16 [3072, 8192], P(('groups', 'seq'), 'chan'), parts along dimension 0
- attn_out: bfloat16 [3072, 64, 128], P(('groups', 'seq'), 'chan'), parts along dimension 0
The draws below stay inside these ranges and needn't reach their ends.
There are 2 independent parts, one for each index of `groups`. The reference program is written for one: setup_inputs(seed, part) draws one part's arguments, and reference() takes and returns one part's arrays. A program takes and returns all parts, laid end to end along the dimension named above; an argument that names none is the same for every part. Nothing has to cross between parts.
All inputs are finite; a program needn't handle non-finite values.
Results may differ from the reference program's by a relative error of at most 0.0045.
Values may be sent and summed in bfloat16 or wider, within the bound.
A program may use at most 64 MiB of HBM per device.

```python
import math
import jax
import jax.numpy as jnp
from jax import lax

TOK_DEV = 384
D_INNER = 8192
HEADS = 128
STATE = 128
BC_GROUPS = 8
CONV = 4
STRETCH = 128
Q_HEADS = 64
KV_HEADS = 8
ATT_DIM = 128
HEAD_DIM = 64
TOKENS = 1536


def draw_dt_in(key, part):
    key_level, key_rough = jax.random.split(jax.random.fold_in(key, 11))
    blocks = TOKENS // TOK_DEV
    level = jnp.exp(jax.random.uniform(key_level, (blocks, 1, 1), jnp.float32, math.log(0.5), math.log(2.0)))
    rough = jax.random.uniform(key_rough, (blocks, TOK_DEV, HEADS), jnp.float32, -0.5, 0.5)
    step_sizes = (level * jnp.exp(rough)).reshape(TOKENS, HEADS)
    return step_sizes + jnp.log(-jnp.expm1(-step_sizes))


def draw_a_log(key, part):
    key_pick, key_fast, key_slow = jax.random.split(jax.random.fold_in(key, 23), 3)
    share = 0.5
    quick = jax.random.uniform(key_pick, (HEADS,), jnp.float32) < share
    fast_rates = jax.random.uniform(key_fast, (HEADS,), jnp.float32, math.log(1.0 / 50.0), math.log(1.0 / 30.0))
    slow_rates = jax.random.uniform(key_slow, (HEADS,), jnp.float32, math.log(0.25), math.log(0.6)) - math.log(TOKENS)
    return jnp.where(quick, fast_rates, slow_rates)


def draw_w_kv(key, part):
    key_scale, key_base = jax.random.split(jax.random.fold_in(key, 31))
    key_scales = jnp.exp(jax.random.uniform(key_scale, (KV_HEADS, ATT_DIM), jnp.float32, math.log(0.3), math.log(3.0)))
    column_scales = jnp.concatenate([key_scales, jnp.ones((KV_HEADS, ATT_DIM), jnp.float32)], axis=-1)
    shape = (D_INNER, KV_HEADS, 2 * ATT_DIM)
    base = jnp.clip(jax.random.normal(key_base, shape, jnp.float32), -4.0, 4.0)
    return (base * column_scales * D_INNER ** (-0.5)).astype(jnp.bfloat16)


def draw_queries(key, part):
    key_width, key_row, key_base = jax.random.split(jax.random.fold_in(key, 37), 3)
    width_scale = jnp.exp(jax.random.uniform(key_width, (Q_HEADS, ATT_DIM), jnp.float32, 0.0, math.log(10.0)))
    row_scale = jnp.exp(jax.random.uniform(key_row, (TOKENS, 1, 1), jnp.float32, math.log(0.1), 0.0))
    shape = (TOKENS, Q_HEADS, ATT_DIM)
    base = jnp.clip(jax.random.normal(key_base, shape, jnp.float32), -4.0, 4.0)
    return (base * width_scale * row_scale).astype(jnp.bfloat16)


def block_levels(stream_key, dims, cuts, least, largest):
    loudness = 1.0
    for axis_at, parts in cuts:
        steps = jax.random.uniform(jax.random.fold_in(jax.random.fold_in(stream_key, 6), axis_at), (parts,), jnp.float32, least / len(cuts), largest / len(cuts))
        loudness = loudness * jnp.repeat(jnp.exp(steps), dims[axis_at] // parts).reshape((-1,) + (1,) * (len(dims) - 1 - axis_at))
    return loudness


def noise(own_key, shape, width, limit, cuts=(), kind=jnp.bfloat16):
    values = jax.random.normal(own_key, shape, jnp.float32) * width
    if len(cuts) > 0:
        values = block_levels(own_key, shape, cuts, -0.22, 0.18) * values
    return jnp.clip(values, min=-limit, max=limit).astype(kind)


def setup_inputs(seed: int = 0, part: int = 0) -> dict:
    key_list = jax.random.split(jax.random.key(seed), 12)
    part_splits = jax.random.split(jax.random.fold_in(key_list[11], part), 12)
    x_in = noise(part_splits[0], (TOKENS, D_INNER), 1.0, 6.0, ((0, 4), (1, 4)))
    b_in = noise(part_splits[1], (TOKENS, BC_GROUPS, STATE), 1.0, 6.0, ((0, 4), (1, 4)))
    c_in = noise(part_splits[2], (TOKENS, BC_GROUPS, STATE), 1.0, 6.0, ((0, 4), (1, 4)))
    dt_in = draw_dt_in(jax.random.fold_in(jax.random.fold_in(key_list[11], part), 71), part)
    a_log = draw_a_log(jax.random.fold_in(key_list[11], 71), part)
    z_in = noise(part_splits[5], (TOKENS, D_INNER), 1.0, 6.0, ((0, 4), (1, 4)))
    conv_x = noise(key_list[6], (CONV, D_INNER), 0.5, 3.0, ((1, 4),), jnp.float32)
    conv_bc = noise(key_list[7], (2, CONV, BC_GROUPS, STATE), 0.5, 3.0, ((2, 4),), jnp.float32)
    norm_gain = jnp.clip(1.0 + 0.15 * jax.random.normal(key_list[8], (D_INNER,), jnp.float32), 0.25, 1.75)
    w_kv = draw_w_kv(jax.random.fold_in(key_list[11], 71), part)
    queries = draw_queries(jax.random.fold_in(jax.random.fold_in(key_list[11], part), 71), part)
    return dict(x_in=x_in, b_in=b_in, c_in=c_in, dt_in=dt_in, a_log=a_log, z_in=z_in, conv_x=conv_x, conv_bc=conv_bc, norm_gain=norm_gain, w_kv=w_kv, queries=queries)


HIGHEST = lax.Precision.HIGHEST

def silu_of(values):
    return values * jax.nn.sigmoid(values)

def rounded(values):
    return lax.optimization_barrier(values.astype(jnp.bfloat16))

def causal_conv(extended, conv_taps, token_count):
    summed = jnp.zeros((token_count,) + extended.shape[1:], jnp.float32)
    for offset in range(conv_taps.shape[0]):
        summed = summed + conv_taps[offset] * extended[offset:offset + token_count]
    return summed

def stretch_scan(x_heads, b_rows, c_rows, step_rows, decay_rates, initial):
    length = STRETCH
    blocks = x_heads.shape[0] // length
    causal_mask = (jnp.arange(length)[:, None] >= jnp.arange(length)[None, :])[:, :, None, None]

    def advance(carried, pieces):
        x_block, b_block, c_block, step_block = pieces
        running = jnp.cumsum(-step_block * decay_rates, axis=0)
        spread = running[:, None] - running[None, :]
        decays = jnp.where(causal_mask, jnp.exp(jnp.where(causal_mask, spread, 0.0)), 0.0)
        intersection = jnp.einsum('tgn,sgn->tsg', c_block, b_block, precision=HIGHEST)
        mixing = decays * intersection[..., None] * step_block[None]
        within = jnp.einsum('tsgh,sghp->tghp', mixing, x_block, precision=HIGHEST)
        before = jnp.einsum('tgn,ghpn->tghp', c_block, carried, precision=HIGHEST) * jnp.exp(running)[..., None]
        tail_weight = jnp.exp(running[-1][None] - running) * step_block
        carried = carried * jnp.exp(running[-1])[..., None, None] + jnp.einsum('sgh,sghp,sgn->ghpn', tail_weight, x_block, b_block, precision=HIGHEST)
        return (carried, within + before)

    def to_blocks(values_in):
        return values_in.reshape((blocks, length) + values_in.shape[1:])
    last_state, outputs = lax.scan(advance, initial, (to_blocks(x_heads), to_blocks(b_rows), to_blocks(c_rows), to_blocks(step_rows)))
    return (outputs.reshape(x_heads.shape), last_state)

def reference(x_in, b_in, c_in, dt_in, a_log, z_in, conv_x, conv_bc, norm_gain, w_kv, queries):
    margin = CONV - 1
    per_group = HEADS // BC_GROUPS

    def padded(values_in):
        zeros = jnp.zeros((margin,) + values_in.shape[1:], jnp.float32)
        return jnp.concatenate([zeros, values_in.astype(jnp.float32)], axis=0)
    x_conv = rounded(silu_of(causal_conv(padded(x_in), conv_x, TOKENS)))
    b_conv = rounded(silu_of(causal_conv(padded(b_in), conv_bc[0], TOKENS)))
    c_conv = rounded(silu_of(causal_conv(padded(c_in), conv_bc[1], TOKENS)))
    step_sizes = jax.nn.softplus(dt_in).reshape(TOKENS, BC_GROUPS, per_group)
    decay_rates = jnp.exp(a_log).reshape(BC_GROUPS, per_group)
    x_heads = x_conv.astype(jnp.float32).reshape(TOKENS, BC_GROUPS, per_group, HEAD_DIM)
    initial = jnp.zeros((BC_GROUPS, per_group, HEAD_DIM, STATE), jnp.float32)
    ssm_out, last_state = stretch_scan(x_heads, b_conv.astype(jnp.float32), c_conv.astype(jnp.float32), step_sizes, decay_rates, initial)
    gated_out = ssm_out.reshape(TOKENS, D_INNER) * silu_of(z_in.astype(jnp.float32))
    grouped = gated_out.reshape(TOKENS, BC_GROUPS, D_INNER // BC_GROUPS)
    normed = grouped * lax.rsqrt(lax.optimization_barrier(jnp.mean(grouped * grouped, axis=-1, keepdims=True)) + 1e-05)
    mixer_out = (normed.reshape(TOKENS, D_INNER) * norm_gain).astype(jnp.bfloat16)
    key_values = jnp.dot(mixer_out, w_kv.reshape(D_INNER, -1), preferred_element_type=jnp.float32)
    key_values = key_values.reshape(TOKENS, KV_HEADS, 2 * ATT_DIM)
    keys_raw = key_values[..., :ATT_DIM]
    key_hat = rounded(keys_raw * lax.rsqrt(lax.optimization_barrier(jnp.mean(keys_raw * keys_raw, axis=-1, keepdims=True)) + 1e-06)).astype(jnp.float32)
    value_b = rounded(key_values[..., ATT_DIM:]).astype(jnp.float32)
    query_f = queries.astype(jnp.float32)
    query_hat = rounded(query_f * lax.rsqrt(lax.optimization_barrier(jnp.mean(query_f * query_f, axis=-1, keepdims=True)) + 1e-06)).astype(jnp.float32)
    group_size = Q_HEADS // KV_HEADS
    query_hat = query_hat.reshape(TOKENS, KV_HEADS, group_size, ATT_DIM)
    query_block = math.gcd(TOKENS, 64)
    key_positions = jnp.arange(TOKENS)
    score_scale = ATT_DIM ** (-0.5)

    def attend_block(block_index):
        first_row = block_index * query_block
        query_rows = lax.dynamic_slice_in_dim(query_hat, first_row, query_block, 0)
        scores = jnp.einsum('tkga,jka->tkgj', query_rows, key_hat, precision=HIGHEST) * score_scale
        query_positions = first_row + jnp.arange(query_block)
        allowed = (query_positions[:, None] >= key_positions[None, :])[:, None, None, :]
        weights = jnp.where(allowed, jnp.exp(scores), 0.0)
        weights_b = rounded(weights).astype(jnp.float32)
        numerator = jnp.einsum('tkgj,jka->tkga', weights_b, value_b, precision=HIGHEST)
        denominator = lax.optimization_barrier(jnp.sum(weights, axis=-1))
        return (numerator / denominator[..., None]).astype(jnp.bfloat16).reshape(query_block, Q_HEADS, ATT_DIM)
    attended = lax.map(attend_block, jnp.arange(TOKENS // query_block))
    attn_out = attended.reshape(TOKENS, Q_HEADS, ATT_DIM)
    return (mixer_out, attn_out)
```

```python
import functools
import math

import jax
import jax.numpy as jnp
from jax import lax
from jax.experimental import pallas as pl
from jax.experimental.pallas import tpu as pltpu
from jax.sharding import PartitionSpec as P

MESH = pl.DeviceIdType.MESH
F32 = jnp.float32
BF16 = jnp.bfloat16
RIM = 16
CORES = 2
WIDE = 256
ROWS = 512


def mm(a, b):
    return jnp.dot(a, b, preferred_element_type=F32)


def contract_rows(a, b):
    return lax.dot_general(a, b, (((0,), (0,)), ((), ())), preferred_element_type=F32)


def contract_lanes(a, b):
    return lax.dot_general(a, b, (((1,), (1,)), ((), ())), preferred_element_type=F32)


def silu(v):
    return v / (1.0 + jnp.exp(-v))


def split2(v):
    high = v.astype(BF16)
    return high, (v - high.astype(F32)).astype(BF16)


def kernel(
    nseq, nchan, nstate, kv_heads,
    x_ref, bc_ref, dt_ref, alog_ref, tx_ref, tbc_ref, gain_ref, z_hbm, w_hbm, q_hbm,
    mix_ref, att_ref,
    zv, wv, qv, rimx, rimbc, xp, bcp, bcv, mask_cb, decay, xs, sl, sin, sout, ybuf, ssq,
    wp, kvp, s1, r1, s2, r2, kvall, qh, acc,
    in_sem, rim_send, rim_recv, st_send, st_recv,
    c1_send, c1_recv, c2_send, c2_recv, kv_send, kv_recv,
):
    tokens, channels = x_ref.shape
    heads = dt_ref.shape[1]
    head_width = channels // heads
    gn = bc_ref.shape[1] // 2
    ngroups = gn // nstate
    nch, _, cw = xs.shape
    per = nch // ngroups
    chg = channels // ngroups
    kvh = kv_heads // nchan
    att = qv.shape[2]
    gs = qv.shape[1] // kvh
    margin = tx_ref.shape[0] - 1
    base = 8 - margin
    nx = nchan // CORES
    me = lax.axis_index("seq")
    chan = lax.axis_index("chan")
    mx = chan // CORES
    core = chan % CORES
    mate = 1 - core
    mate_id = mx * CORES + mate

    def remote(src, dst, ss, rs, where):
        return pltpu.make_async_remote_copy(
            src_ref=src, dst_ref=dst, send_sem=ss, recv_sem=rs, device_id=where, device_id_type=MESH
        )

    z_copy = pltpu.make_async_copy(z_hbm, zv, in_sem.at[0])
    q_copy = pltpu.make_async_copy(q_hbm, qv, in_sem.at[1])
    w_copy = pltpu.make_async_copy(w_hbm, wv, in_sem.at[2])
    z_copy.start()
    q_copy.start()
    w_copy.start()

    barrier = pltpu.get_barrier_semaphore()

    @pl.when(me > 0)
    def _():
        pl.semaphore_signal(barrier, inc=1, device_id={"seq": me - 1}, device_id_type=MESH)

    @pl.when(me < nseq - 1)
    def _():
        pl.semaphore_signal(barrier, inc=1, device_id={"seq": me + 1}, device_id_type=MESH)

    pl.semaphore_signal(barrier, inc=1, device_id={"chan": mate_id}, device_id_type=MESH)
    for off in range(1, nx):
        other = ((mx + off) % nx) * CORES + core
        pl.semaphore_signal(barrier, inc=1, device_id={"chan": other}, device_id_type=MESH)
    pl.semaphore_wait(barrier, nx + jnp.minimum(me, 1) + jnp.minimum(nseq - 1 - me, 1))

    nxt = {"seq": jnp.minimum(me + 1, nseq - 1)}

    def rim_copies():
        return (
            remote(x_ref.at[pl.ds(tokens - RIM, RIM)], rimx, rim_send.at[0], rim_recv.at[0], nxt),
            remote(bc_ref.at[pl.ds(tokens - RIM, RIM)], rimbc, rim_send.at[1], rim_recv.at[1], nxt),
        )

    def state_copy(j):
        return remote(sout.at[j], sin.at[j], st_send.at[j], st_recv.at[j], nxt)

    def kv_copy(src, i):
        return remote(kvall.at[src, i], kvall.at[src, i], kv_send.at[src, i], kv_recv.at[src, i], nxt)

    @pl.when(me < nseq - 1)
    def _():
        for copy in rim_copies():
            copy.start()

    @pl.when(me == 0)
    def _():
        rimx[...] = jnp.zeros_like(rimx)
        rimbc[...] = jnp.zeros_like(rimbc)
        sin[...] = jnp.zeros_like(sin)

    step = jnp.log(1.0 + jnp.exp(dt_ref[...]))
    drop = -step * jnp.exp(alog_ref[...])
    at_row = lax.broadcasted_iota(jnp.int32, (tokens, tokens), 0)
    at_col = lax.broadcasted_iota(jnp.int32, (tokens, tokens), 1)
    causal = at_row >= at_col
    lower = causal.astype(F32).astype(BF16)
    d1, rest = split2(drop)
    d2 = rest
    d3 = (drop - d1.astype(F32) - d2.astype(F32)).astype(BF16)
    running = mm(lower, d1) + mm(lower, d2) + mm(lower, d3)
    e_hi, e_lo = split2(jnp.exp(running))
    w_hi, w_lo = split2(jnp.exp(-running) * step)
    decay[0] = e_hi
    decay[1] = e_lo
    decay[2] = w_hi
    decay[3] = w_lo

    def spread(j):
        head = lax.broadcasted_iota(jnp.int32, (heads, cw), 0) * head_width
        lane = lax.broadcasted_iota(jnp.int32, (heads, cw), 1) + j * cw
        return ((lane >= head) & (lane < head + head_width)).astype(F32).astype(BF16)

    @pl.when(me > 0)
    def _():
        for copy in rim_copies():
            copy.wait_recv()

    bcp[0:8, :] = rimbc[...].astype(F32)[8:16]
    bcp[8 : 8 + tokens, :] = bc_ref[...].astype(F32)
    summed = tbc_ref[0:1, :] * bcp[base : base + tokens, :]
    for k in range(1, margin + 1):
        summed = summed + tbc_ref[k : k + 1, :] * bcp[base + k : base + k + tokens, :]
    bcv[...] = silu(summed).astype(BF16)
    for g in range(ngroups):
        cb = contract_lanes(
            bcv[:, gn + g * nstate : gn + (g + 1) * nstate], bcv[:, g * nstate : (g + 1) * nstate]
        )
        mask_cb[g] = jnp.where(causal, cb, 0.0).astype(BF16)

    def conv_chunk(j, c):
        lanes = pl.ds(pl.multiple_of(j * cw, cw), cw)
        g = j // per
        xp[0:8, :] = rimx[:, lanes].astype(F32)[8:16]
        xp[8 : 8 + tokens, :] = x_ref[:, lanes].astype(F32)
        total = tx_ref[0:1, lanes] * xp[base : base + tokens, :]
        for k in range(1, margin + 1):
            total = total + tx_ref[k : k + 1, lanes] * xp[base + k : base + k + tokens, :]
        conv = silu(total).astype(BF16).astype(F32)
        each = spread(j)
        scaled = (conv * (mm(decay[2], each) + mm(decay[3], each))).astype(BF16)
        xs[j] = scaled
        own = contract_rows(bcv[:, pl.ds(pl.multiple_of(g * nstate, nstate), nstate)], scaled)
        sl[j] = own

        @pl.when(me == 0)
        def _():
            sout[j] = (own * last_decay(j)).astype(BF16)
            state_copy(j).start()

        return c

    def last_decay(j):
        each = spread(j)
        tail = pl.ds(tokens - RIM, RIM)
        return (mm(decay[0, tail, :], each) + mm(decay[1, tail, :], each))[RIM - 1 : RIM, :]

    lax.fori_loop(0, nch, conv_chunk, 0)

    z_copy.wait()
    q_copy.wait()
    w_copy.wait()

    blk = WIDE // kv_heads
    prow = lax.broadcasted_iota(jnp.int32, (WIDE, WIDE), 0)
    pcol = lax.broadcasted_iota(jnp.int32, (WIDE, WIDE), 1)
    perm = (pcol == (prow % blk) * kv_heads + prow // blk).astype(F32).astype(BF16)
    w_parts = channels // blk // nch
    q_rows = tokens // nch

    def filler(j):
        def one(n, c):
            at = j * w_parts + n
            moved = mm(perm, wv[pl.ds(pl.multiple_of(at * WIDE, WIDE), WIDE), :]).astype(BF16)
            for h in range(kv_heads):
                wp[h, pl.ds(pl.multiple_of(at * blk, blk), blk), :] = moved[h * blk : (h + 1) * blk]
            return c

        lax.fori_loop(0, w_parts, one, 0)
        qf = qv[pl.ds(j * q_rows, q_rows)].astype(F32)
        qn = qf * lax.rsqrt(jnp.mean(qf * qf, axis=-1, keepdims=True) + 1e-06)
        for i in range(kvh):
            qh[i, pl.ds(pl.multiple_of(j * q_rows * gs, q_rows * gs), q_rows * gs), :] = (
                qn[:, i * gs : (i + 1) * gs, :].reshape(q_rows * gs, att).astype(BF16)
            )

    def scan_chunk(j, c):
        lanes = pl.ds(pl.multiple_of(j * cw, cw), cw)
        g = j // per

        @pl.when(me > 0)
        def _():
            state_copy(j).wait_recv()

        @pl.when((me > 0) & (me < nseq - 1))
        def _():
            sout[j] = ((sin[j].astype(F32) + sl[j]) * last_decay(j)).astype(BF16)
            state_copy(j).start()

        filler(j)
        each = spread(j)
        gate = silu(zv[:, lanes].astype(F32)) * (mm(decay[0], each) + mm(decay[1], each))
        c_rows = bcv[:, pl.ds(pl.multiple_of(gn + g * nstate, nstate), nstate)]
        y = (mm(mask_cb[g], xs[j]) + mm(c_rows, sin[j])) * gate
        ybuf[j] = y
        sq = y * y
        part = sq[:, 0:128]
        for k in range(1, cw // 128):
            part = part + sq[:, k * 128 : (k + 1) * 128]
        ssq[...] = part + jnp.where(j % per == 0, 0.0, ssq[...])
        return c

    def kv_dot(g, h):
        span = pl.ds(g * chg, chg)
        got = mm(mix_ref[:, span], wp[h, span, :])
        return got if g == 0 else kvp[h] + got

    ssq[...] = jnp.zeros_like(ssq)
    for g in range(ngroups):
        lax.fori_loop(g * per, (g + 1) * per, scan_chunk, 0)
        scale = lax.rsqrt(jnp.sum(ssq[...], axis=-1, keepdims=True) / chg + 1e-05)

        def norm_chunk(j, c):
            lanes = pl.ds(pl.multiple_of(j * cw, cw), cw)
            mix_ref[:, lanes] = (ybuf[j] * scale * gain_ref[0:1, lanes]).astype(BF16)
            return c

        lax.fori_loop(g * per, (g + 1) * per, norm_chunk, 0)
        if g < ngroups - 1:

            def kv_part(h, c):
                kvp[h] = kv_dot(g, h)
                return c

            lax.fori_loop(0, kv_heads, kv_part, 0)

    last = ngroups - 1

    def core_copy(i, cx):
        return remote(
            s1.at[i, cx], r1.at[i, cx], c1_send.at[i, cx], c1_recv.at[i, cx], {"chan": mate_id}
        )

    def chip_copy(i, to, slot):
        return remote(
            s2.at[i, to], r2.at[i, slot], c2_send.at[i, to], c2_recv.at[i, slot],
            {"chan": to * CORES + core},
        )

    for i in range(kvh):

        def to_mate(n, c, i=i):
            cx = (mx + 1 + n) % nx
            s1[i, cx] = kv_dot(last, (cx * CORES + mate) * kvh + i).astype(BF16)
            core_copy(i, cx).start()
            return c

        lax.fori_loop(0, nx, to_mate, 0)
    for i in range(kvh):

        def to_chip(n, c, i=i):
            cx = (mx + 1 + n) % nx
            h = (cx * CORES + core) * kvh + i
            mine = kv_dot(last, h)
            core_copy(i, cx).wait_recv()
            both = mine + r1[i, cx].astype(F32)
            kvp[h] = both

            @pl.when(n < nx - 1)
            def _():
                s2[i, cx] = both.astype(BF16)
                chip_copy(i, cx, mx).start()

            return c

        lax.fori_loop(0, nx, to_chip, 0)

    factor = att ** (-0.5) * math.log2(math.e)
    rows = min(ROWS, tokens * gs)
    parts = tokens * gs // rows

    def attend(i, src, own):
        keys = kvall[src, i, :, 0:att]
        values = jnp.concatenate([kvall[src, i, :, att:], jnp.ones((tokens, att), BF16)], axis=1)

        def part(p, c):
            span = pl.ds(pl.multiple_of(p * rows, rows), rows)
            weights = jnp.exp2(contract_lanes(qh[i, span, :], keys) * factor)
            if own:
                row = lax.broadcasted_iota(jnp.int32, (rows, tokens), 0) + p * rows
                col = lax.broadcasted_iota(jnp.int32, (rows, tokens), 1) * gs
                weights = jnp.where(row >= col, weights, 0.0)
            got = mm(weights.astype(BF16), values)
            acc[i, span, :] = got if own else acc[i, span, :] + got
            return c

        lax.fori_loop(0, parts, part, 0)

    for i in range(kvh):
        total = kvp[chan * kvh + i]
        for off in range(1, nx):
            cx = (mx + off) % nx
            chip_copy(i, cx, cx).wait_recv()
            total = total + r2[i, cx].astype(F32)
        key = total[:, 0:att]
        key = key * lax.rsqrt(jnp.mean(key * key, axis=-1, keepdims=True) + 1e-06)
        kvall[me, i, :, 0:att] = key.astype(BF16)
        kvall[me, i, :, att:] = total[:, att:].astype(BF16)

        @pl.when(me < nseq - 1)
        def _(i=i):
            kv_copy(me, i).start()

        attend(i, me, True)

    def earlier(s, c):
        src = me - s
        for i in range(kvh):
            kv_copy(src, i).wait_recv()

            @pl.when(me < nseq - 1)
            def _(i=i):
                kv_copy(src, i).start()

            attend(i, src, False)
        return c

    lax.fori_loop(1, me + 1, earlier, 0)

    out_rows = tokens // nch

    def finish(p, c):
        span = pl.ds(pl.multiple_of(p * out_rows * gs, out_rows * gs), out_rows * gs)
        done = [
            (acc[i, span, 0:att] / acc[i, span, att:]).reshape(out_rows, gs, att) for i in range(kvh)
        ]
        whole = done[0] if kvh == 1 else jnp.concatenate(done, axis=1)
        att_ref[pl.ds(p * out_rows, out_rows)] = whole.astype(BF16)
        return c

    lax.fori_loop(0, nch, finish, 0)

    for i in range(kvh):
        for off in range(nx):
            core_copy(i, (mx + off) % nx).wait_send()
        for off in range(1, nx):
            chip_copy(i, (mx + off) % nx, mx).wait_send()

    @pl.when(me < nseq - 1)
    def _():
        for copy in rim_copies():
            copy.wait_send()
        for j in range(nch):
            state_copy(j).wait_send()

        def sent(s, c):
            for i in range(kvh):
                kv_copy(s, i).wait_send()
            return c

        lax.fori_loop(0, me + 1, sent, 0)


def on_device(nseq, nchan, x_in, b_in, c_in, dt_in, a_log, z_in, conv_x, conv_bc, norm_gain, w_kv, queries):
    tokens, channels = x_in.shape
    _, ngroups, nstate = b_in.shape
    gn = ngroups * nstate
    heads = dt_in.shape[1]
    kv_heads, kw = w_kv.shape[1:]
    q_heads, att = queries.shape[1:]
    kvh = kv_heads // nchan
    gs = q_heads // kvh
    taps = conv_x.shape[0]
    cw = min(WIDE, channels // ngroups)
    nch = channels // cw
    nx = nchan // CORES
    bc = jnp.concatenate([b_in.reshape(tokens, gn), c_in.reshape(tokens, gn)], axis=1)
    tbc = jnp.concatenate([conv_bc[0].reshape(taps, gn), conv_bc[1].reshape(taps, gn)], axis=1)
    vmem = pl.BlockSpec(memory_space=pltpu.VMEM)
    hbm = pl.BlockSpec(memory_space=pl.ANY)
    dma = pltpu.SemaphoreType.DMA
    return pl.pallas_call(
        functools.partial(kernel, nseq, nchan, nstate, kv_heads),
        out_shape=(
            jax.ShapeDtypeStruct((tokens, channels), BF16),
            jax.ShapeDtypeStruct((tokens, q_heads, att), BF16),
        ),
        in_specs=[vmem] * 7 + [hbm] * 3,
        out_specs=(vmem, vmem),
        scratch_shapes=[
            pltpu.VMEM((tokens, channels), BF16),
            pltpu.VMEM((channels * kv_heads, kw), BF16),
            pltpu.VMEM((tokens, q_heads, att), BF16),
            pltpu.VMEM((RIM, channels), BF16),
            pltpu.VMEM((RIM, 2 * gn), BF16),
            pltpu.VMEM((tokens + 8, cw), F32),
            pltpu.VMEM((tokens + 8, 2 * gn), F32),
            pltpu.VMEM((tokens, 2 * gn), BF16),
            pltpu.VMEM((ngroups, tokens, tokens), BF16),
            pltpu.VMEM((4, tokens, heads), BF16),
            pltpu.VMEM((nch, tokens, cw), BF16),
            pltpu.VMEM((nch, nstate, cw), F32),
            pltpu.VMEM((nch, nstate, cw), BF16),
            pltpu.VMEM((nch, nstate, cw), BF16),
            pltpu.VMEM((nch, tokens, cw), F32),
            pltpu.VMEM((tokens, 128), F32),
            pltpu.VMEM((kv_heads, channels, kw), BF16),
            pltpu.VMEM((kv_heads, tokens, kw), F32),
            pltpu.VMEM((kvh, nx, tokens, kw), BF16),
            pltpu.VMEM((kvh, nx, tokens, kw), BF16),
            pltpu.VMEM((kvh, nx, tokens, kw), BF16),
            pltpu.VMEM((kvh, nx, tokens, kw), BF16),
            pltpu.VMEM((nseq, kvh, tokens, kw), BF16),
            pltpu.VMEM((kvh, tokens * gs, att), BF16),
            pltpu.VMEM((kvh, tokens * gs, 2 * att), F32),
            dma((3,)),
            dma((2,)),
            dma((2,)),
            dma((nch,)),
            dma((nch,)),
            dma((kvh, nx)),
            dma((kvh, nx)),
            dma((kvh, nx)),
            dma((kvh, nx)),
            dma((nseq, kvh)),
            dma((nseq, kvh)),
        ],
        compiler_params=pltpu.CompilerParams(
            collective_id=0, has_side_effects=True, vmem_limit_bytes=62 * 1024 * 1024
        ),
        name="mixer_attention",
    )(
        x_in, bc, dt_in, a_log.reshape(1, heads), conv_x, tbc, norm_gain.reshape(1, channels),
        z_in, w_kv.reshape(channels * kv_heads, kw), queries,
    )


def solution(mesh):
    return jax.shard_map(
        functools.partial(on_device, mesh.shape["seq"], mesh.shape["chan"]),
        mesh=mesh,
        in_specs=(
            P(("groups", "seq"), "chan"),
            P(("groups", "seq"), "chan", None),
            P(("groups", "seq"), "chan", None),
            P(("groups", "seq"), "chan"),
            P("chan"),
            P(("groups", "seq"), "chan"),
            P(None, "chan"),
            P(None, None, "chan", None),
            P("chan"),
            P("chan", None, None),
            P(("groups", "seq"), "chan", None),
        ),
        out_specs=(P(("groups", "seq"), "chan"), P(("groups", "seq"), "chan", None)),
        check_vma=False,
    )
```

```python
import functools
import math

import jax
import jax.numpy as jnp
from jax import lax
from jax.experimental import pallas as pl
from jax.experimental.pallas import tpu as pltpu
from jax.sharding import PartitionSpec as P

MESH = pl.DeviceIdType.MESH
F32 = jnp.float32
BF16 = jnp.bfloat16
RIM = 16
CORES = 2
WIDE = 256
ROWS = 512


def mm(a, b):
    return jnp.dot(a, b, preferred_element_type=F32)


def contract_rows(a, b):
    return lax.dot_general(a, b, (((0,), (0,)), ((), ())), preferred_element_type=F32)


def contract_lanes(a, b):
    return lax.dot_general(a, b, (((1,), (1,)), ((), ())), preferred_element_type=F32)


def silu(v):
    return v / (1.0 + jnp.exp(-v))


def split2(v):
    high = v.astype(BF16)
    return high, (v - high.astype(F32)).astype(BF16)


def kernel(
    nseq, nchan, nstate, kv_heads,
    x_ref, b_ref, c_ref, dt_ref, alog_ref, tx_ref, tbc_ref, gain_ref, z_hbm, w_hbm, q_hbm,
    mix_ref, att_ref,
    zv, wv, qv, rimx, rimb, rimc, xp, bcp, bcv, mask_cb, decay, xs, sl, sin, sout, ybuf, ssq,
    wp, kvp, s1, r1, s2, r2, kvall, qh, acc,
    in_sem, rim_send, rim_recv, st_send, st_recv,
    c1_send, c1_recv, c2_send, c2_recv, kv_send, kv_recv,
):
    tokens, channels = x_ref.shape
    heads = dt_ref.shape[0]
    head_width = channels // heads
    ngroups = b_ref.shape[1]
    gn = ngroups * nstate
    nch, _, cw = xs.shape
    per = nch // ngroups
    chg = channels // ngroups
    kvh = kv_heads // nchan
    att = qv.shape[2]
    gs = qv.shape[1] // kvh
    margin = tx_ref.shape[0] - 1
    base = 8 - margin
    nx = nchan // CORES
    me = lax.axis_index("seq")
    chan = lax.axis_index("chan")
    mx = chan // CORES
    core = chan % CORES
    mate = 1 - core
    mate_id = mx * CORES + mate

    def remote(src, dst, ss, rs, where):
        return pltpu.make_async_remote_copy(
            src_ref=src, dst_ref=dst, send_sem=ss, recv_sem=rs, device_id=where, device_id_type=MESH
        )

    z_copy = pltpu.make_async_copy(z_hbm, zv, in_sem.at[0])
    q_copy = pltpu.make_async_copy(q_hbm, qv, in_sem.at[1])
    w_copy = pltpu.make_async_copy(w_hbm, wv, in_sem.at[2])
    z_copy.start()
    q_copy.start()
    w_copy.start()

    barrier = pltpu.get_barrier_semaphore()

    @pl.when(me > 0)
    def _():
        pl.semaphore_signal(barrier, inc=1, device_id={"seq": me - 1}, device_id_type=MESH)

    @pl.when(me < nseq - 1)
    def _():
        pl.semaphore_signal(barrier, inc=1, device_id={"seq": me + 1}, device_id_type=MESH)

    pl.semaphore_signal(barrier, inc=1, device_id={"chan": mate_id}, device_id_type=MESH)
    for off in range(1, nx):
        other = ((mx + off) % nx) * CORES + core
        pl.semaphore_signal(barrier, inc=1, device_id={"chan": other}, device_id_type=MESH)
    pl.semaphore_wait(barrier, nx + jnp.minimum(me, 1) + jnp.minimum(nseq - 1 - me, 1))

    nxt = {"seq": jnp.minimum(me + 1, nseq - 1)}

    def rim_copies():
        return (
            remote(x_ref.at[pl.ds(tokens - RIM, RIM)], rimx, rim_send.at[0], rim_recv.at[0], nxt),
            remote(b_ref.at[pl.ds(tokens - RIM, RIM)], rimb, rim_send.at[1], rim_recv.at[1], nxt),
            remote(c_ref.at[pl.ds(tokens - RIM, RIM)], rimc, rim_send.at[2], rim_recv.at[2], nxt),
        )

    def state_copy(j):
        return remote(sout.at[j], sin.at[j], st_send.at[j], st_recv.at[j], nxt)

    def kv_copy(src, i):
        return remote(kvall.at[src, i], kvall.at[src, i], kv_send.at[src, i], kv_recv.at[src, i], nxt)

    @pl.when(me < nseq - 1)
    def _():
        for copy in rim_copies():
            copy.start()

    @pl.when(me == 0)
    def _():
        rimx[...] = jnp.zeros_like(rimx)
        rimb[...] = jnp.zeros_like(rimb)
        rimc[...] = jnp.zeros_like(rimc)
        sin[...] = jnp.zeros_like(sin)

    step = jnp.log(1.0 + jnp.exp(dt_ref[...]))
    same = lax.broadcasted_iota(jnp.int32, (heads, heads), 0) == lax.broadcasted_iota(
        jnp.int32, (heads, heads), 1
    )
    rates = jnp.sum(jnp.where(same, jnp.exp(alog_ref[...]), 0.0), axis=1, keepdims=True)
    drop = -step * rates
    at_row = lax.broadcasted_iota(jnp.int32, (tokens, tokens), 0)
    at_col = lax.broadcasted_iota(jnp.int32, (tokens, tokens), 1)
    causal = at_row >= at_col
    lower = causal.astype(F32).astype(BF16)
    d1, rest = split2(drop)
    d2 = rest
    d3 = (drop - d1.astype(F32) - d2.astype(F32)).astype(BF16)
    running = contract_lanes(d1, lower) + contract_lanes(d2, lower) + contract_lanes(d3, lower)
    e_hi, e_lo = split2(jnp.exp(running))
    w_hi, w_lo = split2(jnp.exp(-running) * step)
    decay[0] = e_hi
    decay[1] = e_lo
    decay[2] = w_hi
    decay[3] = w_lo

    def spread(j):
        head = lax.broadcasted_iota(jnp.int32, (heads, cw), 0) * head_width
        lane = lax.broadcasted_iota(jnp.int32, (heads, cw), 1) + j * cw
        return ((lane >= head) & (lane < head + head_width)).astype(F32).astype(BF16)

    @pl.when(me > 0)
    def _():
        for copy in rim_copies():
            copy.wait_recv()

    for which, (ref, rim) in enumerate(((b_ref, rimb), (c_ref, rimc))):
        full = ref[...].astype(F32)
        ahead = rim[...].astype(F32)
        for g in range(ngroups):
            lanes = slice(which * gn + g * nstate, which * gn + (g + 1) * nstate)
            bcp[0:8, lanes] = ahead[8:16, g, :]
            bcp[8 : 8 + tokens, lanes] = full[:, g, :]
            summed = tbc_ref[which, 0, g : g + 1, :] * bcp[base : base + tokens, lanes]
            for k in range(1, margin + 1):
                taps = tbc_ref[which, k, g : g + 1, :]
                summed = summed + taps * bcp[base + k : base + k + tokens, lanes]
            bcv[:, lanes] = silu(summed).astype(BF16)
    for g in range(ngroups):
        cb = contract_lanes(
            bcv[:, gn + g * nstate : gn + (g + 1) * nstate], bcv[:, g * nstate : (g + 1) * nstate]
        )
        mask_cb[g] = jnp.where(causal, cb, 0.0).astype(BF16)

    def conv_chunk(j, c):
        lanes = pl.ds(pl.multiple_of(j * cw, cw), cw)
        g = j // per
        xp[0:8, :] = rimx[:, lanes].astype(F32)[8:16]
        xp[8 : 8 + tokens, :] = x_ref[:, lanes].astype(F32)
        total = tx_ref[0:1, lanes] * xp[base : base + tokens, :]
        for k in range(1, margin + 1):
            total = total + tx_ref[k : k + 1, lanes] * xp[base + k : base + k + tokens, :]
        conv = silu(total).astype(BF16).astype(F32)
        each = spread(j)
        scaled = (conv * (contract_rows(decay[2], each) + contract_rows(decay[3], each))).astype(BF16)
        xs[j] = scaled
        own = contract_rows(bcv[:, pl.ds(pl.multiple_of(g * nstate, nstate), nstate)], scaled)
        sl[j] = own

        @pl.when(me == 0)
        def _():
            sout[j] = (own * last_decay(j)).astype(BF16)
            state_copy(j).start()

        return c

    def last_decay(j):
        each = spread(j)
        tail = slice(tokens - 128, tokens)
        got = contract_rows(decay[0, :, tail], each) + contract_rows(decay[1, :, tail], each)
        return got[127:128, :]

    lax.fori_loop(0, nch, conv_chunk, 0)

    z_copy.wait()
    q_copy.wait()
    w_copy.wait()

    blk = WIDE // kv_heads
    prow = lax.broadcasted_iota(jnp.int32, (WIDE, WIDE), 0)
    pcol = lax.broadcasted_iota(jnp.int32, (WIDE, WIDE), 1)
    perm = (pcol == (prow % blk) * kv_heads + prow // blk).astype(F32).astype(BF16)
    w_parts = channels // blk // nch
    q_rows = tokens // nch

    def filler(j):
        for n in range(w_parts):
            at = j * w_parts + n
            moved = mm(perm, wv[pl.ds(pl.multiple_of(at * WIDE, WIDE), WIDE), :]).astype(BF16)
            for h in range(kv_heads):
                wp[h, pl.ds(pl.multiple_of(at * blk, blk), blk), :] = moved[h * blk : (h + 1) * blk]
        qf = qv[pl.ds(j * q_rows, q_rows)].astype(F32)
        qn = qf * lax.rsqrt(jnp.mean(qf * qf, axis=-1, keepdims=True) + 1e-06)
        for i in range(kvh):
            qh[i, pl.ds(pl.multiple_of(j * q_rows * gs, q_rows * gs), q_rows * gs), :] = (
                qn[:, i * gs : (i + 1) * gs, :].reshape(q_rows * gs, att).astype(BF16)
            )

    def scan_chunk(j, c):
        lanes = pl.ds(pl.multiple_of(j * cw, cw), cw)
        g = j // per

        @pl.when(me > 0)
        def _():
            state_copy(j).wait_recv()

        @pl.when((me > 0) & (me < nseq - 1))
        def _():
            sout[j] = ((sin[j].astype(F32) + sl[j]) * last_decay(j)).astype(BF16)
            state_copy(j).start()

        filler(j)
        each = spread(j)
        gate = silu(zv[:, lanes].astype(F32)) * (contract_rows(decay[0], each) + contract_rows(decay[1], each))
        c_rows = bcv[:, pl.ds(pl.multiple_of(gn + g * nstate, nstate), nstate)]
        y = (mm(mask_cb[g], xs[j]) + mm(c_rows, sin[j])) * gate
        ybuf[j] = y
        sq = y * y
        part = sq[:, 0:128]
        for k in range(1, cw // 128):
            part = part + sq[:, k * 128 : (k + 1) * 128]
        ssq[...] = part + jnp.where(j % per == 0, 0.0, ssq[...])
        return c

    def kv_dot(g, h):
        span = pl.ds(g * chg, chg)
        got = mm(mix_ref[:, span], wp[h, span, :])
        return got if g == 0 else kvp[h] + got

    ssq[...] = jnp.zeros_like(ssq)
    acc[...] = jnp.zeros_like(acc)
    for g in range(ngroups):
        lax.fori_loop(g * per, (g + 1) * per, scan_chunk, 0)
        scale = lax.rsqrt(jnp.sum(ssq[...], axis=-1, keepdims=True) / chg + 1e-05)

        def norm_chunk(j, c):
            lanes = pl.ds(pl.multiple_of(j * cw, cw), cw)
            mix_ref[:, lanes] = (ybuf[j] * scale * gain_ref[0:1, lanes]).astype(BF16)
            return c

        lax.fori_loop(g * per, (g + 1) * per, norm_chunk, 0)
        if g < ngroups - 1:

            def kv_part(h, c):
                kvp[h] = kv_dot(g, h)
                return c

            lax.fori_loop(0, kv_heads, kv_part, 0)

    last = ngroups - 1

    def core_copy(i, cx):
        return remote(
            s1.at[i, cx], r1.at[i, cx], c1_send.at[i, cx], c1_recv.at[i, cx], {"chan": mate_id}
        )

    def chip_copy(i, to, slot):
        return remote(
            s2.at[i, to], r2.at[i, slot], c2_send.at[i, to], c2_recv.at[i, slot],
            {"chan": to * CORES + core},
        )

    for i in range(kvh):

        def to_mate(n, c, i=i):
            cx = (mx + 1 + n) % nx
            s1[i, cx] = kv_dot(last, (cx * CORES + mate) * kvh + i).astype(BF16)
            core_copy(i, cx).start()
            return c

        lax.fori_loop(0, nx, to_mate, 0)

        def to_chip(n, c, i=i):
            cx = (mx + 1 + n) % nx
            h = (cx * CORES + core) * kvh + i
            mine = kv_dot(last, h)
            core_copy(i, cx).wait_recv()
            both = mine + r1[i, cx].astype(F32)
            kvp[h] = both

            @pl.when(n < nx - 1)
            def _():
                s2[i, cx] = both.astype(BF16)
                chip_copy(i, cx, mx).start()

            return c

        lax.fori_loop(0, nx, to_chip, 0)

    factor = att ** (-0.5) * math.log2(math.e)
    rows = min(ROWS, tokens * gs)
    parts = tokens * gs // rows

    def attend(i, src, own):
        keys = kvall[src, i, :, 0:att]
        values = jnp.concatenate([kvall[src, i, :, att:], jnp.ones((tokens, att), BF16)], axis=1)

        def part(p, c):
            span = pl.ds(pl.multiple_of(p * rows, rows), rows)
            weights = jnp.exp2(contract_lanes(qh[i, span, :], keys) * factor)
            if own:
                row = lax.broadcasted_iota(jnp.int32, (rows, tokens), 0) + p * rows
                col = lax.broadcasted_iota(jnp.int32, (rows, tokens), 1) * gs
                weights = jnp.where(row >= col, weights, 0.0)
            got = mm(weights.astype(BF16), values)
            acc[i, span, :] = acc[i, span, :] + got
            return c

        lax.fori_loop(0, parts, part, 0)

    def earlier(src, c):
        for i in range(kvh):
            kv_copy(src, i).wait_recv()

            @pl.when(me < nseq - 1)
            def _(i=i):
                kv_copy(src, i).start()

            attend(i, src, False)
        return c

    before = jnp.minimum(me, max(nseq - 2, 0))
    lax.fori_loop(0, before, earlier, 0)
    for i in range(kvh):
        total = kvp[chan * kvh + i]
        for off in range(1, nx):
            cx = (mx + off) % nx
            chip_copy(i, cx, cx).wait_recv()
            total = total + r2[i, cx].astype(F32)
        key = total[:, 0:att]
        key = key * lax.rsqrt(jnp.mean(key * key, axis=-1, keepdims=True) + 1e-06)
        kvall[me, i, :, 0:att] = key.astype(BF16)
        kvall[me, i, :, att:] = total[:, att:].astype(BF16)

        @pl.when(me < nseq - 1)
        def _(i=i):
            kv_copy(me, i).start()

        attend(i, me, True)
    lax.fori_loop(before, me, earlier, 0)

    out_rows = tokens // nch

    def finish(p, c):
        span = pl.ds(pl.multiple_of(p * out_rows * gs, out_rows * gs), out_rows * gs)
        done = [
            (acc[i, span, 0:att] / acc[i, span, att:]).reshape(out_rows, gs, att) for i in range(kvh)
        ]
        whole = done[0] if kvh == 1 else jnp.concatenate(done, axis=1)
        att_ref[pl.ds(p * out_rows, out_rows)] = whole.astype(BF16)
        return c

    lax.fori_loop(0, nch, finish, 0)

    for i in range(kvh):
        for off in range(nx):
            core_copy(i, (mx + off) % nx).wait_send()
        for off in range(1, nx):
            chip_copy(i, (mx + off) % nx, mx).wait_send()

    @pl.when(me < nseq - 1)
    def _():
        for copy in rim_copies():
            copy.wait_send()
        for j in range(nch):
            state_copy(j).wait_send()

        def sent(s, c):
            for i in range(kvh):
                kv_copy(s, i).wait_send()
            return c

        lax.fori_loop(0, me + 1, sent, 0)


def on_device(nseq, nchan, x_in, b_in, c_in, dt_in, a_log, z_in, conv_x, conv_bc, norm_gain, w_kv, queries):
    tokens, channels = x_in.shape
    _, ngroups, nstate = b_in.shape
    gn = ngroups * nstate
    heads = dt_in.shape[1]
    kv_heads, kw = w_kv.shape[1:]
    q_heads, att = queries.shape[1:]
    kvh = kv_heads // nchan
    gs = q_heads // kvh
    cw = min(WIDE, channels // ngroups)
    nch = channels // cw
    nx = nchan // CORES
    vmem = pl.BlockSpec(memory_space=pltpu.VMEM)
    hbm = pl.BlockSpec(memory_space=pl.ANY)
    dma = pltpu.SemaphoreType.DMA
    return pl.pallas_call(
        functools.partial(kernel, nseq, nchan, nstate, kv_heads),
        out_shape=(
            jax.ShapeDtypeStruct((tokens, channels), BF16),
            jax.ShapeDtypeStruct((tokens, q_heads, att), BF16),
        ),
        in_specs=[vmem] * 8 + [hbm] * 3,
        out_specs=(vmem, vmem),
        scratch_shapes=[
            pltpu.VMEM((tokens, channels), BF16),
            pltpu.VMEM((channels * kv_heads, kw), BF16),
            pltpu.VMEM((tokens, q_heads, att), BF16),
            pltpu.VMEM((RIM, channels), BF16),
            pltpu.VMEM((RIM, ngroups, nstate), BF16),
            pltpu.VMEM((RIM, ngroups, nstate), BF16),
            pltpu.VMEM((tokens + 8, cw), F32),
            pltpu.VMEM((tokens + 8, 2 * gn), F32),
            pltpu.VMEM((tokens, 2 * gn), BF16),
            pltpu.VMEM((ngroups, tokens, tokens), BF16),
            pltpu.VMEM((4, heads, tokens), BF16),
            pltpu.VMEM((nch, tokens, cw), BF16),
            pltpu.VMEM((nch, nstate, cw), F32),
            pltpu.VMEM((nch, nstate, cw), BF16),
            pltpu.VMEM((nch, nstate, cw), BF16),
            pltpu.VMEM((nch, tokens, cw), F32),
            pltpu.VMEM((tokens, 128), F32),
            pltpu.VMEM((kv_heads, channels, kw), BF16),
            pltpu.VMEM((kv_heads, tokens, kw), F32),
            pltpu.VMEM((kvh, nx, tokens, kw), BF16),
            pltpu.VMEM((kvh, nx, tokens, kw), BF16),
            pltpu.VMEM((kvh, nx, tokens, kw), BF16),
            pltpu.VMEM((kvh, nx, tokens, kw), BF16),
            pltpu.VMEM((nseq, kvh, tokens, kw), BF16),
            pltpu.VMEM((kvh, tokens * gs, att), BF16),
            pltpu.VMEM((kvh, tokens * gs, 2 * att), F32),
            dma((3,)),
            dma((3,)),
            dma((3,)),
            dma((nch,)),
            dma((nch,)),
            dma((kvh, nx)),
            dma((kvh, nx)),
            dma((kvh, nx)),
            dma((kvh, nx)),
            dma((nseq, kvh)),
            dma((nseq, kvh)),
        ],
        compiler_params=pltpu.CompilerParams(
            collective_id=0, has_side_effects=True, vmem_limit_bytes=62 * 1024 * 1024
        ),
        name="mixer_attention",
    )(
        x_in, b_in, c_in, dt_in.T, a_log.reshape(1, heads), conv_x, conv_bc, norm_gain.reshape(1, channels),
        z_in, w_kv.reshape(channels * kv_heads, kw), queries,
    )


def solution(mesh):
    return jax.shard_map(
        functools.partial(on_device, mesh.shape["seq"], mesh.shape["chan"]),
        mesh=mesh,
        in_specs=(
            P(("groups", "seq"), "chan"),
            P(("groups", "seq"), "chan", None),
            P(("groups", "seq"), "chan", None),
            P(("groups", "seq"), "chan"),
            P("chan"),
            P(("groups", "seq"), "chan"),
            P(None, "chan"),
            P(None, None, "chan", None),
            P("chan"),
            P("chan", None, None),
            P(("groups", "seq"), "chan", None),
        ),
        out_specs=(P(("groups", "seq"), "chan"), P(("groups", "seq"), "chan", None)),
        check_vma=False,
    )
```

```python
import functools
import math

import jax
import jax.numpy as jnp
from jax import lax
from jax.experimental import pallas as pl
from jax.experimental.pallas import tpu as pltpu
from jax.sharding import PartitionSpec as P

MESH = pl.DeviceIdType.MESH
F32 = jnp.float32
BF16 = jnp.bfloat16
RIM = 16
CORES = 2
WIDE = 256
ROWS = 512


def mm(a, b):
    return jnp.dot(a, b, preferred_element_type=F32)


def contract_rows(a, b):
    return lax.dot_general(a, b, (((0,), (0,)), ((), ())), preferred_element_type=F32)


def contract_lanes(a, b):
    return lax.dot_general(a, b, (((1,), (1,)), ((), ())), preferred_element_type=F32)


def silu(v):
    half = 0.5 * v
    return half + half * jnp.tanh(half)


def split2(v):
    high = v.astype(BF16)
    return high, (v - high.astype(F32)).astype(BF16)


def kernel(
    nseq, nchan, nstate, kv_heads,
    x_ref, b_ref, c_ref, dt_ref, alog_ref, tx_ref, tbc_ref, gain_ref, z_hbm, w_hbm, q_hbm,
    mix_out, att_ref,
    mix_ref, zv, wv, qv, rimx, rimb, rimc, xp, bcp, bcv, mask_cb, decay, xs, sl, sin, sout, ybuf, ssq,
    wp, kvp, s1, r1, s2, r2, kvall, qh, acc,
    in_sem, rim_send, rim_recv, st_send, st_recv,
    c1_send, c1_recv, c2_send, c2_recv, kv_send, kv_recv,
):
    tokens, channels = x_ref.shape
    heads = dt_ref.shape[0]
    head_width = channels // heads
    ngroups = b_ref.shape[1]
    gn = ngroups * nstate
    nch, _, cw = xs.shape
    per = nch // ngroups
    chg = channels // ngroups
    kvh = kv_heads // nchan
    att = qv.shape[2]
    gs = qv.shape[1] // kvh
    margin = tx_ref.shape[0] - 1
    base = 8 - margin
    nx = nchan // CORES
    me = lax.axis_index("seq")
    chan = lax.axis_index("chan")
    mx = chan // CORES
    core = chan % CORES
    mate = 1 - core
    mate_id = mx * CORES + mate

    def remote(src, dst, ss, rs, where):
        return pltpu.make_async_remote_copy(
            src_ref=src, dst_ref=dst, send_sem=ss, recv_sem=rs, device_id=where, device_id_type=MESH
        )

    z_copy = pltpu.make_async_copy(z_hbm, zv, in_sem.at[0])
    q_copy = pltpu.make_async_copy(q_hbm, qv, in_sem.at[1])
    w_copy = pltpu.make_async_copy(w_hbm, wv, in_sem.at[2])
    z_copy.start()
    q_copy.start()
    w_copy.start()

    barrier = pltpu.get_barrier_semaphore()

    @pl.when(me > 0)
    def _():
        pl.semaphore_signal(barrier, inc=1, device_id={"seq": me - 1}, device_id_type=MESH)

    @pl.when(me < nseq - 1)
    def _():
        pl.semaphore_signal(barrier, inc=1, device_id={"seq": me + 1}, device_id_type=MESH)

    pl.semaphore_signal(barrier, inc=1, device_id={"chan": mate_id}, device_id_type=MESH)
    for off in range(1, nx):
        other = ((mx + off) % nx) * CORES + core
        pl.semaphore_signal(barrier, inc=1, device_id={"chan": other}, device_id_type=MESH)
    pl.semaphore_wait(barrier, nx + jnp.minimum(me, 1) + jnp.minimum(nseq - 1 - me, 1))

    nxt = {"seq": jnp.minimum(me + 1, nseq - 1)}

    def rim_copies():
        return (
            remote(x_ref.at[pl.ds(tokens - RIM, RIM)], rimx, rim_send.at[0], rim_recv.at[0], nxt),
            remote(b_ref.at[pl.ds(tokens - RIM, RIM)], rimb, rim_send.at[1], rim_recv.at[1], nxt),
            remote(c_ref.at[pl.ds(tokens - RIM, RIM)], rimc, rim_send.at[2], rim_recv.at[2], nxt),
        )

    def state_copy(j):
        return remote(sout.at[j], sin.at[j], st_send.at[j], st_recv.at[j], nxt)

    def kv_copy(src, i):
        return remote(kvall.at[src, i], kvall.at[src, i], kv_send.at[src, i], kv_recv.at[src, i], nxt)

    @pl.when(me < nseq - 1)
    def _():
        for copy in rim_copies():
            copy.start()

    @pl.when(me == 0)
    def _():
        rimx[...] = jnp.zeros_like(rimx)
        rimb[...] = jnp.zeros_like(rimb)
        rimc[...] = jnp.zeros_like(rimc)
        sin[...] = jnp.zeros_like(sin)

    step = jnp.log(1.0 + jnp.exp(dt_ref[...]))
    same = lax.broadcasted_iota(jnp.int32, (heads, heads), 0) == lax.broadcasted_iota(
        jnp.int32, (heads, heads), 1
    )
    rates = jnp.sum(jnp.where(same, jnp.exp(alog_ref[...]), 0.0), axis=1, keepdims=True)
    drop = -step * rates
    at_row = lax.broadcasted_iota(jnp.int32, (tokens, tokens), 0)
    at_col = lax.broadcasted_iota(jnp.int32, (tokens, tokens), 1)
    causal = at_row >= at_col
    lower = causal.astype(F32).astype(BF16)
    d1, rest = split2(drop)
    d2 = rest
    d3 = (drop - d1.astype(F32) - d2.astype(F32)).astype(BF16)
    running = contract_lanes(d1, lower) + contract_lanes(d2, lower) + contract_lanes(d3, lower)
    e_hi, e_lo = split2(jnp.exp(running))
    w_hi, w_lo = split2(jnp.exp(-running) * step)
    decay[0] = e_hi
    decay[1] = e_lo
    decay[2] = w_hi
    decay[3] = w_lo

    def spread(j):
        head = lax.broadcasted_iota(jnp.int32, (heads, cw), 0) * head_width
        lane = lax.broadcasted_iota(jnp.int32, (heads, cw), 1) + j * cw
        return ((lane >= head) & (lane < head + head_width)).astype(F32).astype(BF16)

    @pl.when(me > 0)
    def _():
        for copy in rim_copies():
            copy.wait_recv()

    for which, (ref, rim) in enumerate(((b_ref, rimb), (c_ref, rimc))):
        full = ref[...].astype(F32)
        ahead = rim[...].astype(F32)
        for g in range(ngroups):
            lanes = slice(which * gn + g * nstate, which * gn + (g + 1) * nstate)
            bcp[0:8, lanes] = ahead[8:16, g, :]
            bcp[8 : 8 + tokens, lanes] = full[:, g, :]
            summed = tbc_ref[which, 0, g : g + 1, :] * bcp[base : base + tokens, lanes]
            for k in range(1, margin + 1):
                taps = tbc_ref[which, k, g : g + 1, :]
                summed = summed + taps * bcp[base + k : base + k + tokens, lanes]
            bcv[:, lanes] = silu(summed).astype(BF16)
    for g in range(ngroups):
        cb = contract_lanes(
            bcv[:, gn + g * nstate : gn + (g + 1) * nstate], bcv[:, g * nstate : (g + 1) * nstate]
        )
        mask_cb[g] = jnp.where(causal, cb, 0.0).astype(BF16)

    pair = 2 if per % 2 == 0 else 1

    def conv_one(j, slot):
        lanes = pl.ds(pl.multiple_of(j * cw, cw), cw)
        g = j // per
        xp[slot, 0:8, :] = rimx[:, lanes].astype(F32)[8:16]
        xp[slot, 8 : 8 + tokens, :] = x_ref[:, lanes].astype(F32)
        total = tx_ref[0:1, lanes] * xp[slot, base : base + tokens, :]
        for k in range(1, margin + 1):
            total = total + tx_ref[k : k + 1, lanes] * xp[slot, base + k : base + k + tokens, :]
        conv = silu(total).astype(BF16).astype(F32)
        each = spread(j)
        scaled = (conv * (contract_rows(decay[2], each) + contract_rows(decay[3], each))).astype(BF16)
        xs[j] = scaled
        own = contract_rows(bcv[:, pl.ds(pl.multiple_of(g * nstate, nstate), nstate)], scaled)
        sl[j] = own * last_decay(j)

    def conv_chunks(p, c):
        for k in range(pair):
            conv_one(p * pair + k, k)

        @pl.when(me == 0)
        def _():
            for k in range(pair):
                j = p * pair + k
                sout[j] = sl[j].astype(BF16)
                state_copy(j).start()

        return c

    def last_decay(j):
        each = spread(j)
        tail = slice(tokens - 128, tokens)
        got = contract_rows(decay[0, :, tail], each) + contract_rows(decay[1, :, tail], each)
        return got[127:128, :]

    lax.fori_loop(0, nch // pair, conv_chunks, 0)

    z_copy.wait()
    w_copy.wait()

    blk = WIDE // kv_heads
    prow = lax.broadcasted_iota(jnp.int32, (WIDE, WIDE), 0)
    pcol = lax.broadcasted_iota(jnp.int32, (WIDE, WIDE), 1)
    perm = (pcol == (prow % blk) * kv_heads + prow // blk).astype(F32).astype(BF16)
    w_parts = channels // blk // nch
    q_rows = tokens // nch

    def weights_part(j):
        for n in range(w_parts):
            at = j * w_parts + n
            moved = mm(perm, wv[pl.ds(pl.multiple_of(at * WIDE, WIDE), WIDE), :]).astype(BF16)
            for h in range(kv_heads):
                wp[h, pl.ds(pl.multiple_of(at * blk, blk), blk), :] = moved[h * blk : (h + 1) * blk]

    def query_part(j, c):
        qf = qv[pl.ds(j * q_rows, q_rows)].astype(F32)
        qn = qf * lax.rsqrt(jnp.mean(qf * qf, axis=-1, keepdims=True) + 1e-06)
        for i in range(kvh):
            qh[i, pl.ds(pl.multiple_of(j * q_rows * gs, q_rows * gs), q_rows * gs), :] = (
                qn[:, i * gs : (i + 1) * gs, :].reshape(q_rows * gs, att).astype(BF16)
            )

        return c

    def scan_chunks(p, c):
        for k in range(pair):
            j = p * pair + k

            @pl.when(me > 0)
            def _(j=j):
                state_copy(j).wait_recv()

            @pl.when((me > 0) & (me < nseq - 1))
            def _(j=j):
                sout[j] = (sin[j].astype(F32) * last_decay(j) + sl[j]).astype(BF16)
                state_copy(j).start()

        sums = jnp.where((p * pair) % per == 0, 0.0, ssq[...])
        for k in range(pair):
            j = p * pair + k
            lanes = pl.ds(pl.multiple_of(j * cw, cw), cw)
            g = j // per
            weights_part(j)
            each = spread(j)
            gate = silu(zv[:, lanes].astype(F32)) * (
                contract_rows(decay[0], each) + contract_rows(decay[1], each)
            )
            c_rows = bcv[:, pl.ds(pl.multiple_of(gn + g * nstate, nstate), nstate)]
            y = (mm(mask_cb[g], xs[j]) + mm(c_rows, sin[j])) * gate
            ybuf[j] = y
            sq = y * y
            for m in range(cw // 128):
                sums = sums + sq[:, m * 128 : (m + 1) * 128]
        ssq[...] = sums
        return c

    def kv_dot(g, h):
        span = pl.ds(g * chg, chg)
        got = mm(mix_ref[:, span], wp[h, span, :])
        return got if g == 0 else kvp[h] + got

    ssq[...] = jnp.zeros_like(ssq)
    for g in range(ngroups):
        lax.fori_loop(g * per // pair, (g + 1) * per // pair, scan_chunks, 0)
        scale = lax.rsqrt(jnp.sum(ssq[...], axis=-1, keepdims=True) / chg + 1e-05)

        def norm_chunk(j, c):
            lanes = pl.ds(pl.multiple_of(j * cw, cw), cw)
            mix_ref[:, lanes] = (ybuf[j] * scale * gain_ref[0:1, lanes]).astype(BF16)
            return c

        lax.fori_loop(g * per, (g + 1) * per, norm_chunk, 0)
        if g < ngroups - 1:

            def kv_part(h, c):
                kvp[h] = kv_dot(g, h)
                return c

            lax.fori_loop(0, kv_heads, kv_part, 0)

    mix_copy = pltpu.make_async_copy(mix_ref, mix_out, in_sem.at[3])
    mix_copy.start()

    last = ngroups - 1

    def core_copy(i, cx):
        return remote(
            s1.at[i, cx], r1.at[i, cx], c1_send.at[i, cx], c1_recv.at[i, cx], {"chan": mate_id}
        )

    def chip_copy(i, to, slot):
        return remote(
            s2.at[i, to], r2.at[i, slot], c2_send.at[i, to], c2_recv.at[i, slot],
            {"chan": to * CORES + core},
        )

    for i in range(kvh):

        def to_mate(n, c, i=i):
            cx = (mx + 1 + n) % nx
            s1[i, cx] = kv_dot(last, (cx * CORES + mate) * kvh + i).astype(BF16)
            core_copy(i, cx).start()
            return c

        lax.fori_loop(0, nx, to_mate, 0)

        def to_chip(n, c, i=i):
            cx = (mx + 1 + n) % nx
            h = (cx * CORES + core) * kvh + i
            mine = kv_dot(last, h)
            core_copy(i, cx).wait_recv()
            both = mine + r1[i, cx].astype(F32)
            kvp[h] = both

            @pl.when(n < nx - 1)
            def _():
                s2[i, cx] = both.astype(BF16)
                chip_copy(i, cx, mx).start()

            return c

        lax.fori_loop(0, nx, to_chip, 0)

    factor = att ** (-0.5) * math.log2(math.e)
    rows = min(ROWS, tokens * gs)
    parts = tokens * gs // rows

    def attend(i, src, own):
        keys = kvall[src, i, :, 0:att]
        values = jnp.concatenate([kvall[src, i, :, att:], jnp.ones((tokens, att), BF16)], axis=1)

        def part(p, c):
            span = pl.ds(pl.multiple_of(p * rows, rows), rows)
            weights = jnp.exp2(contract_lanes(qh[i, span, :], keys) * factor)
            if own:
                row = lax.broadcasted_iota(jnp.int32, (rows, tokens), 0) + p * rows
                col = lax.broadcasted_iota(jnp.int32, (rows, tokens), 1) * gs
                weights = jnp.where(row >= col, weights, 0.0)
            got = mm(weights.astype(BF16), values)
            acc[i, span, :] = got if own else acc[i, span, :] + got
            return c

        lax.fori_loop(0, parts, part, 0)

    def earlier(back, c):
        src = me - back
        for i in range(kvh):
            kv_copy(src, i).wait_recv()

            @pl.when(me < nseq - 1)
            def _(i=i):
                kv_copy(src, i).start()

            attend(i, src, False)
        return c

    q_copy.wait()
    lax.fori_loop(0, nch, query_part, 0)
    for i in range(kvh):
        total = kvp[chan * kvh + i]
        for off in range(1, nx):
            cx = (mx + off) % nx
            chip_copy(i, cx, cx).wait_recv()
            total = total + r2[i, cx].astype(F32)
        key = total[:, 0:att]
        key = key * lax.rsqrt(jnp.mean(key * key, axis=-1, keepdims=True) + 1e-06)
        kvall[me, i, :, 0:att] = key.astype(BF16)
        kvall[me, i, :, att:] = total[:, att:].astype(BF16)

        @pl.when(me < nseq - 1)
        def _(i=i):
            kv_copy(me, i).start()

        attend(i, me, True)
    lax.fori_loop(1, me + 1, earlier, 0)

    out_rows = tokens // nch

    def finish(p, c):
        span = pl.ds(pl.multiple_of(p * out_rows * gs, out_rows * gs), out_rows * gs)
        done = [
            (acc[i, span, 0:att] / acc[i, span, att:]).reshape(out_rows, gs, att) for i in range(kvh)
        ]
        whole = done[0] if kvh == 1 else jnp.concatenate(done, axis=1)
        att_ref[pl.ds(p * out_rows, out_rows)] = whole.astype(BF16)
        return c

    lax.fori_loop(0, nch, finish, 0)

    mix_copy.wait()
    for i in range(kvh):
        for off in range(nx):
            core_copy(i, (mx + off) % nx).wait_send()
        for off in range(1, nx):
            chip_copy(i, (mx + off) % nx, mx).wait_send()

    @pl.when(me < nseq - 1)
    def _():
        for copy in rim_copies():
            copy.wait_send()
        for j in range(nch):
            state_copy(j).wait_send()

        def sent(s, c):
            for i in range(kvh):
                kv_copy(s, i).wait_send()
            return c

        lax.fori_loop(0, me + 1, sent, 0)


def on_device(nseq, nchan, x_in, b_in, c_in, dt_in, a_log, z_in, conv_x, conv_bc, norm_gain, w_kv, queries):
    tokens, channels = x_in.shape
    _, ngroups, nstate = b_in.shape
    gn = ngroups * nstate
    heads = dt_in.shape[1]
    kv_heads, kw = w_kv.shape[1:]
    q_heads, att = queries.shape[1:]
    kvh = kv_heads // nchan
    gs = q_heads // kvh
    cw = min(WIDE, channels // ngroups)
    nch = channels // cw
    nx = nchan // CORES
    vmem = pl.BlockSpec(memory_space=pltpu.VMEM)
    hbm = pl.BlockSpec(memory_space=pl.ANY)
    dma = pltpu.SemaphoreType.DMA
    return pl.pallas_call(
        functools.partial(kernel, nseq, nchan, nstate, kv_heads),
        out_shape=(
            jax.ShapeDtypeStruct((tokens, channels), BF16),
            jax.ShapeDtypeStruct((tokens, q_heads, att), BF16),
        ),
        in_specs=[vmem] * 8 + [hbm] * 3,
        out_specs=(hbm, vmem),
        scratch_shapes=[
            pltpu.VMEM((tokens, channels), BF16),
            pltpu.VMEM((tokens, channels), BF16),
            pltpu.VMEM((channels * kv_heads, kw), BF16),
            pltpu.VMEM((tokens, q_heads, att), BF16),
            pltpu.VMEM((RIM, channels), BF16),
            pltpu.VMEM((RIM, ngroups, nstate), BF16),
            pltpu.VMEM((RIM, ngroups, nstate), BF16),
            pltpu.VMEM((2, tokens + 8, cw), F32),
            pltpu.VMEM((tokens + 8, 2 * gn), F32),
            pltpu.VMEM((tokens, 2 * gn), BF16),
            pltpu.VMEM((ngroups, tokens, tokens), BF16),
            pltpu.VMEM((4, heads, tokens), BF16),
            pltpu.VMEM((nch, tokens, cw), BF16),
            pltpu.VMEM((nch, nstate, cw), F32),
            pltpu.VMEM((nch, nstate, cw), BF16),
            pltpu.VMEM((nch, nstate, cw), BF16),
            pltpu.VMEM((nch, tokens, cw), F32),
            pltpu.VMEM((tokens, 128), F32),
            pltpu.VMEM((kv_heads, channels, kw), BF16),
            pltpu.VMEM((kv_heads, tokens, kw), F32),
            pltpu.VMEM((kvh, nx, tokens, kw), BF16),
            pltpu.VMEM((kvh, nx, tokens, kw), BF16),
            pltpu.VMEM((kvh, nx, tokens, kw), BF16),
            pltpu.VMEM((kvh, nx, tokens, kw), BF16),
            pltpu.VMEM((nseq, kvh, tokens, kw), BF16),
            pltpu.VMEM((kvh, tokens * gs, att), BF16),
            pltpu.VMEM((kvh, tokens * gs, 2 * att), F32),
            dma((4,)),
            dma((3,)),
            dma((3,)),
            dma((nch,)),
            dma((nch,)),
            dma((kvh, nx)),
            dma((kvh, nx)),
            dma((kvh, nx)),
            dma((kvh, nx)),
            dma((nseq, kvh)),
            dma((nseq, kvh)),
        ],
        compiler_params=pltpu.CompilerParams(
            collective_id=0, has_side_effects=True, vmem_limit_bytes=62 * 1024 * 1024
        ),
        name="mixer_attention",
    )(
        x_in, b_in, c_in, dt_in.T, a_log.reshape(1, heads), conv_x, conv_bc, norm_gain.reshape(1, channels),
        z_in, w_kv.reshape(channels * kv_heads, kw), queries,
    )


def solution(mesh):
    return jax.shard_map(
        functools.partial(on_device, mesh.shape["seq"], mesh.shape["chan"]),
        mesh=mesh,
        in_specs=(
            P(("groups", "seq"), "chan"),
            P(("groups", "seq"), "chan", None),
            P(("groups", "seq"), "chan", None),
            P(("groups", "seq"), "chan"),
            P("chan"),
            P(("groups", "seq"), "chan"),
            P(None, "chan"),
            P(None, None, "chan", None),
            P("chan"),
            P("chan", None, None),
            P(("groups", "seq"), "chan", None),
        ),
        out_specs=(P(("groups", "seq"), "chan"), P(("groups", "seq"), "chan", None)),
        check_vma=False,
    )
```

```python
import functools
import math

import jax
import jax.numpy as jnp
from jax import lax
from jax.experimental import pallas as pl
from jax.experimental.pallas import tpu as pltpu
from jax.sharding import PartitionSpec as P

MESH = pl.DeviceIdType.MESH
F32 = jnp.float32
BF16 = jnp.bfloat16
RIM = 16
CORES = 2
WIDE = 256
ROWS = 512
HALVES = 2
OUT_PARTS = 4


def mm(a, b):
    return jnp.dot(a, b, preferred_element_type=F32)


def contract_rows(a, b):
    return lax.dot_general(a, b, (((0,), (0,)), ((), ())), preferred_element_type=F32)


def contract_lanes(a, b):
    return lax.dot_general(a, b, (((1,), (1,)), ((), ())), preferred_element_type=F32)


def silu(v):
    half = 0.5 * v
    return half + half * jnp.tanh(half)


def split2(v):
    high = v.astype(BF16)
    return high, (v - high.astype(F32)).astype(BF16)


def kernel(
    nseq, nchan, nstate, kv_heads,
    x_ref, b_ref, c_ref, dt_ref, alog_ref, tx_ref, tbc_ref, gain_ref, z_hbm, w_hbm, q_hbm,
    mix_out, att_ref,
    mix_ref, zv, wv, qv, rimx, rimb, rimc, xp, bcp, bcv, mask_cb, decay, xs, sl, sin, sout, ybuf, ssq,
    wp, kvp, s1, r1, s2, r2, kvall, qh, acc,
    in_sem, rim_send, rim_recv, st_send, st_recv,
    c1_send, c1_recv, c2_send, c2_recv, kv_send, kv_recv,
):
    tokens, channels = x_ref.shape
    heads = dt_ref.shape[0]
    head_width = channels // heads
    ngroups = b_ref.shape[1]
    gn = ngroups * nstate
    nch, _, cw = xs.shape
    per = nch // ngroups
    chg = channels // ngroups
    kvh = kv_heads // nchan
    att = qv.shape[2]
    gs = qv.shape[1] // kvh
    margin = tx_ref.shape[0] - 1
    base = 8 - margin
    nx = nchan // CORES
    me = lax.axis_index("seq")
    chan = lax.axis_index("chan")
    mx = chan // CORES
    core = chan % CORES
    mate = 1 - core
    mate_id = mx * CORES + mate

    def remote(src, dst, ss, rs, where):
        return pltpu.make_async_remote_copy(
            src_ref=src, dst_ref=dst, send_sem=ss, recv_sem=rs, device_id=where, device_id_type=MESH
        )

    z_copy = pltpu.make_async_copy(z_hbm, zv, in_sem.at[0])
    q_copy = pltpu.make_async_copy(q_hbm, qv, in_sem.at[1])
    w_copy = pltpu.make_async_copy(w_hbm, wv, in_sem.at[2])
    z_copy.start()
    q_copy.start()
    w_copy.start()

    barrier = pltpu.get_barrier_semaphore()

    @pl.when(me > 0)
    def _():
        pl.semaphore_signal(barrier, inc=1, device_id={"seq": me - 1}, device_id_type=MESH)

    @pl.when(me < nseq - 1)
    def _():
        pl.semaphore_signal(barrier, inc=1, device_id={"seq": me + 1}, device_id_type=MESH)

    pl.semaphore_signal(barrier, inc=1, device_id={"chan": mate_id}, device_id_type=MESH)
    for off in range(1, nx):
        other = ((mx + off) % nx) * CORES + core
        pl.semaphore_signal(barrier, inc=1, device_id={"chan": other}, device_id_type=MESH)
    pl.semaphore_wait(barrier, nx + jnp.minimum(me, 1) + jnp.minimum(nseq - 1 - me, 1))

    nxt = {"seq": jnp.minimum(me + 1, nseq - 1)}

    def rim_copies():
        return (
            remote(x_ref.at[pl.ds(tokens - RIM, RIM)], rimx, rim_send.at[0], rim_recv.at[0], nxt),
            remote(b_ref.at[pl.ds(tokens - RIM, RIM)], rimb, rim_send.at[1], rim_recv.at[1], nxt),
            remote(c_ref.at[pl.ds(tokens - RIM, RIM)], rimc, rim_send.at[2], rim_recv.at[2], nxt),
        )

    def state_copy(j):
        return remote(sout.at[j], sin.at[j], st_send.at[j], st_recv.at[j], nxt)

    def kv_copy(src, i, f):
        half = tokens // HALVES
        block = kvall.at[src, i, pl.ds(f * half, half)]
        return remote(block, block, kv_send.at[src, i, f], kv_recv.at[src, i, f], nxt)

    @pl.when(me < nseq - 1)
    def _():
        for copy in rim_copies():
            copy.start()

    @pl.when(me == 0)
    def _():
        rimx[...] = jnp.zeros_like(rimx)
        rimb[...] = jnp.zeros_like(rimb)
        rimc[...] = jnp.zeros_like(rimc)
        sin[...] = jnp.zeros_like(sin)

    step = jnp.log(1.0 + jnp.exp(dt_ref[...]))
    same = lax.broadcasted_iota(jnp.int32, (heads, heads), 0) == lax.broadcasted_iota(
        jnp.int32, (heads, heads), 1
    )
    rates = jnp.sum(jnp.where(same, jnp.exp(alog_ref[...]), 0.0), axis=1, keepdims=True)
    drop = -step * rates
    at_row = lax.broadcasted_iota(jnp.int32, (tokens, tokens), 0)
    at_col = lax.broadcasted_iota(jnp.int32, (tokens, tokens), 1)
    causal = at_row >= at_col
    lower = causal.astype(F32).astype(BF16)
    d1, rest = split2(drop)
    d2 = rest
    d3 = (drop - d1.astype(F32) - d2.astype(F32)).astype(BF16)
    running = contract_lanes(d1, lower) + contract_lanes(d2, lower) + contract_lanes(d3, lower)
    e_hi, e_lo = split2(jnp.exp(running))
    w_hi, w_lo = split2(jnp.exp(-running) * step)
    decay[0] = e_hi
    decay[1] = e_lo
    decay[2] = w_hi
    decay[3] = w_lo

    def spread(j):
        head = lax.broadcasted_iota(jnp.int32, (heads, cw), 0) * head_width
        lane = lax.broadcasted_iota(jnp.int32, (heads, cw), 1) + j * cw
        return ((lane >= head) & (lane < head + head_width)).astype(F32).astype(BF16)

    @pl.when(me > 0)
    def _():
        for copy in rim_copies():
            copy.wait_recv()

    for which, (ref, rim) in enumerate(((b_ref, rimb), (c_ref, rimc))):
        full = ref[...].astype(F32)
        ahead = rim[...].astype(F32)
        for g in range(ngroups):
            lanes = slice(which * gn + g * nstate, which * gn + (g + 1) * nstate)
            bcp[0:8, lanes] = ahead[8:16, g, :]
            bcp[8 : 8 + tokens, lanes] = full[:, g, :]
            summed = tbc_ref[which, 0, g : g + 1, :] * bcp[base : base + tokens, lanes]
            for k in range(1, margin + 1):
                taps = tbc_ref[which, k, g : g + 1, :]
                summed = summed + taps * bcp[base + k : base + k + tokens, lanes]
            bcv[:, lanes] = silu(summed).astype(BF16)
    for g in range(ngroups):
        cb = contract_lanes(
            bcv[:, gn + g * nstate : gn + (g + 1) * nstate], bcv[:, g * nstate : (g + 1) * nstate]
        )
        mask_cb[g] = jnp.where(causal, cb, 0.0).astype(BF16)

    pair = 2 if per % 2 == 0 else 1

    def conv_one(j, slot):
        lanes = pl.ds(pl.multiple_of(j * cw, cw), cw)
        g = j // per
        xp[slot, 0:8, :] = rimx[:, lanes].astype(F32)[8:16]
        xp[slot, 8 : 8 + tokens, :] = x_ref[:, lanes].astype(F32)
        total = tx_ref[0:1, lanes] * xp[slot, base : base + tokens, :]
        for k in range(1, margin + 1):
            total = total + tx_ref[k : k + 1, lanes] * xp[slot, base + k : base + k + tokens, :]
        conv = silu(total).astype(BF16).astype(F32)
        each = spread(j)
        scaled = (conv * (contract_rows(decay[2], each) + contract_rows(decay[3], each))).astype(BF16)
        xs[j] = scaled
        own = contract_rows(bcv[:, pl.ds(pl.multiple_of(g * nstate, nstate), nstate)], scaled)
        sl[j] = own * last_decay(j)

    pairs = nch // pair
    ahead_by = 2

    def take_states(p):
        for k in range(pair):
            j = p * pair + k
            state_copy(j).wait_recv()

            @pl.when(me < nseq - 1)
            def _(j=j):
                sout[j] = (sin[j].astype(F32) * last_decay(j) + sl[j]).astype(BF16)
                state_copy(j).start()

    def conv_chunks(p, c):
        for k in range(pair):
            conv_one(p * pair + k, k)

        @pl.when(me == 0)
        def _():
            for k in range(pair):
                j = p * pair + k
                sout[j] = sl[j].astype(BF16)
                state_copy(j).start()

        @pl.when((me == 1) & (p >= ahead_by))
        def _():
            take_states(p - ahead_by)

        return c

    def last_decay(j):
        each = spread(j)
        tail = slice(tokens - 128, tokens)
        got = contract_rows(decay[0, :, tail], each) + contract_rows(decay[1, :, tail], each)
        return got[127:128, :]

    lax.fori_loop(0, nch // pair, conv_chunks, 0)

    z_copy.wait()
    w_copy.wait()

    blk = WIDE // kv_heads
    prow = lax.broadcasted_iota(jnp.int32, (WIDE, WIDE), 0)
    pcol = lax.broadcasted_iota(jnp.int32, (WIDE, WIDE), 1)
    perm = (pcol == (prow % blk) * kv_heads + prow // blk).astype(F32).astype(BF16)
    w_parts = channels // blk // nch
    q_rows = tokens // nch

    def weights_part(j):
        for n in range(w_parts):
            at = j * w_parts + n
            moved = mm(perm, wv[pl.ds(pl.multiple_of(at * WIDE, WIDE), WIDE), :]).astype(BF16)
            for h in range(kv_heads):
                wp[h, pl.ds(pl.multiple_of(at * blk, blk), blk), :] = moved[h * blk : (h + 1) * blk]

    def query_part(j, c):
        qf = qv[pl.ds(j * q_rows, q_rows)].astype(F32)
        qn = qf * lax.rsqrt(jnp.mean(qf * qf, axis=-1, keepdims=True) + 1e-06)
        for i in range(kvh):
            qh[i, pl.ds(pl.multiple_of(j * q_rows * gs, q_rows * gs), q_rows * gs), :] = (
                qn[:, i * gs : (i + 1) * gs, :].reshape(q_rows * gs, att).astype(BF16)
            )

        return c

    def scan_chunks(p, c):
        @pl.when((me > 1) | ((me == 1) & (p >= pairs - ahead_by)))
        def _():
            take_states(p)

        sums = jnp.where((p * pair) % per == 0, 0.0, ssq[...])
        for k in range(pair):
            j = p * pair + k
            lanes = pl.ds(pl.multiple_of(j * cw, cw), cw)
            g = j // per
            weights_part(j)
            each = spread(j)
            gate = silu(zv[:, lanes].astype(F32)) * (
                contract_rows(decay[0], each) + contract_rows(decay[1], each)
            )
            c_rows = bcv[:, pl.ds(pl.multiple_of(gn + g * nstate, nstate), nstate)]
            y = (mm(mask_cb[g], xs[j]) + mm(c_rows, sin[j])) * gate
            ybuf[j] = y
            sq = y * y
            for m in range(cw // 128):
                sums = sums + sq[:, m * 128 : (m + 1) * 128]
        ssq[...] = sums
        return c

    def kv_dot(g, h):
        span = pl.ds(g * chg, chg)
        got = mm(mix_ref[:, span], wp[h, span, :])
        return got if g == 0 else kvp[h] + got

    ssq[...] = jnp.zeros_like(ssq)
    for g in range(ngroups):
        lax.fori_loop(g * per // pair, (g + 1) * per // pair, scan_chunks, 0)
        scale = lax.rsqrt(jnp.sum(ssq[...], axis=-1, keepdims=True) / chg + 1e-05)

        def norm_chunk(j, c):
            lanes = pl.ds(pl.multiple_of(j * cw, cw), cw)
            mix_ref[:, lanes] = (ybuf[j] * scale * gain_ref[0:1, lanes]).astype(BF16)
            return c

        lax.fori_loop(g * per, (g + 1) * per, norm_chunk, 0)
        if g < ngroups - 1:

            def kv_part(h, c):
                kvp[h] = kv_dot(g, h)
                return c

            lax.fori_loop(0, kv_heads, kv_part, 0)

    mix_copy = pltpu.make_async_copy(mix_ref, mix_out, in_sem.at[3])
    mix_copy.start()

    last = ngroups - 1

    def core_copy(i, cx):
        return remote(
            s1.at[i, cx], r1.at[i, cx], c1_send.at[i, cx], c1_recv.at[i, cx], {"chan": mate_id}
        )

    half = tokens // HALVES

    def chip_copy(i, to, slot, f):
        span = pl.ds(f * half, half)
        return remote(
            s2.at[i, to, span], r2.at[i, slot, span], c2_send.at[i, to, f], c2_recv.at[i, slot, f],
            {"chan": to * CORES + core},
        )

    for i in range(kvh):

        def to_mate(n, c, i=i):
            cx = (mx + 1 + n) % nx
            s1[i, cx] = kv_dot(last, (cx * CORES + mate) * kvh + i).astype(BF16)
            core_copy(i, cx).start()
            return c

        lax.fori_loop(0, nx, to_mate, 0)

        def to_chip(n, c, i=i):
            cx = (mx + 1 + n) % nx
            h = (cx * CORES + core) * kvh + i
            mine = kv_dot(last, h)
            core_copy(i, cx).wait_recv()
            both = mine + r1[i, cx].astype(F32)
            kvp[h] = both

            @pl.when(n < nx - 1)
            def _():
                s2[i, cx] = both.astype(BF16)
                for f in range(HALVES):
                    chip_copy(i, cx, mx, f).start()

            return c

        lax.fori_loop(0, nx, to_chip, 0)

    factor = att ** (-0.5) * math.log2(math.e)
    rows = min(ROWS, tokens * gs)
    parts = tokens * gs // rows

    def attend(i, src, own):
        keys = kvall[src, i, :, 0:att]
        values = jnp.concatenate([kvall[src, i, :, att:], jnp.ones((tokens, att), BF16)], axis=1)

        def part(p, c):
            span = pl.ds(pl.multiple_of(p * rows, rows), rows)
            weights = jnp.exp2(contract_lanes(qh[i, span, :], keys) * factor)
            if own:
                row = lax.broadcasted_iota(jnp.int32, (rows, tokens), 0) + p * rows
                col = lax.broadcasted_iota(jnp.int32, (rows, tokens), 1) * gs
                weights = jnp.where(row >= col, weights, 0.0)
            got = mm(weights.astype(BF16), values)
            acc[i, span, :] = got if own else acc[i, span, :] + got
            return c

        lax.fori_loop(0, parts, part, 0)

    out_rows = tokens // nch

    def finish(i):
        def part(p, c):
            span = pl.ds(pl.multiple_of(p * out_rows * gs, out_rows * gs), out_rows * gs)
            done = acc[i, span, 0:att] / acc[i, span, att:]
            att_ref[pl.ds(p * out_rows, out_rows), i * gs : (i + 1) * gs, :] = done.astype(
                BF16
            ).reshape(out_rows, gs, att)
            return c

        lax.fori_loop(0, nch, part, 0)

    def earlier(back, c):
        src = me - back
        for i in range(kvh):
            for f in range(HALVES):
                kv_copy(src, i, f).wait_recv()

                @pl.when(me < nseq - 1)
                def _(i=i, f=f):
                    kv_copy(src, i, f).start()

            attend(i, src, False)

            @pl.when(back == me)
            def _(i=i):
                finish(i)

        return c

    q_copy.wait()
    lax.fori_loop(0, nch, query_part, 0)
    for i in range(kvh):
        for f in range(HALVES):
            span = slice(f * half, (f + 1) * half)
            total = kvp[chan * kvh + i, span]
            for off in range(1, nx):
                cx = (mx + off) % nx
                chip_copy(i, cx, cx, f).wait_recv()
                total = total + r2[i, cx, span].astype(F32)
            key = total[:, 0:att]
            key = key * lax.rsqrt(jnp.mean(key * key, axis=-1, keepdims=True) + 1e-06)
            kvall[me, i, span, 0:att] = key.astype(BF16)
            kvall[me, i, span, att:] = total[:, att:].astype(BF16)

            @pl.when(me < nseq - 1)
            def _(i=i, f=f):
                kv_copy(me, i, f).start()

        attend(i, me, True)

        @pl.when(me == 0)
        def _(i=i):
            finish(i)

    lax.fori_loop(1, me + 1, earlier, 0)

    mix_copy.wait()
    for i in range(kvh):
        for off in range(nx):
            core_copy(i, (mx + off) % nx).wait_send()
        for off in range(1, nx):
            for f in range(HALVES):
                chip_copy(i, (mx + off) % nx, mx, f).wait_send()

    @pl.when(me < nseq - 1)
    def _():
        for copy in rim_copies():
            copy.wait_send()
        for j in range(nch):
            state_copy(j).wait_send()

        def sent(s, c):
            for i in range(kvh):
                for f in range(HALVES):
                    kv_copy(s, i, f).wait_send()
            return c

        lax.fori_loop(0, me + 1, sent, 0)


def hand_out(a_in, b_in, a_out, b_out, sem):
    rows = a_in.shape[0] // OUT_PARTS
    copies = []
    for n in range(OUT_PARTS):
        span = pl.ds(n * rows, rows)
        copies.append(pltpu.make_async_copy(a_in.at[span], a_out.at[span], sem.at[0, n]))
        copies.append(pltpu.make_async_copy(b_in.at[span], b_out.at[span], sem.at[1, n]))
    for copy in copies:
        copy.start()
    for copy in copies:
        copy.wait()


def on_device(nseq, nchan, x_in, b_in, c_in, dt_in, a_log, z_in, conv_x, conv_bc, norm_gain, w_kv, queries):
    tokens, channels = x_in.shape
    _, ngroups, nstate = b_in.shape
    gn = ngroups * nstate
    heads = dt_in.shape[1]
    kv_heads, kw = w_kv.shape[1:]
    q_heads, att = queries.shape[1:]
    kvh = kv_heads // nchan
    gs = q_heads // kvh
    cw = min(WIDE, channels // ngroups)
    nch = channels // cw
    nx = nchan // CORES
    vmem = pl.BlockSpec(memory_space=pltpu.VMEM)
    hbm = pl.BlockSpec(memory_space=pl.ANY)
    dma = pltpu.SemaphoreType.DMA
    mixed, attended = pl.pallas_call(
        functools.partial(kernel, nseq, nchan, nstate, kv_heads),
        out_shape=(
            jax.ShapeDtypeStruct((tokens, channels), BF16),
            jax.ShapeDtypeStruct((tokens, q_heads, att), BF16),
        ),
        in_specs=[vmem] * 8 + [hbm] * 3,
        out_specs=(hbm, vmem),
        scratch_shapes=[
            pltpu.VMEM((tokens, channels), BF16),
            pltpu.VMEM((tokens, channels), BF16),
            pltpu.VMEM((channels * kv_heads, kw), BF16),
            pltpu.VMEM((tokens, q_heads, att), BF16),
            pltpu.VMEM((RIM, channels), BF16),
            pltpu.VMEM((RIM, ngroups, nstate), BF16),
            pltpu.VMEM((RIM, ngroups, nstate), BF16),
            pltpu.VMEM((2, tokens + 8, cw), F32),
            pltpu.VMEM((tokens + 8, 2 * gn), F32),
            pltpu.VMEM((tokens, 2 * gn), BF16),
            pltpu.VMEM((ngroups, tokens, tokens), BF16),
            pltpu.VMEM((4, heads, tokens), BF16),
            pltpu.VMEM((nch, tokens, cw), BF16),
            pltpu.VMEM((nch, nstate, cw), F32),
            pltpu.VMEM((nch, nstate, cw), BF16),
            pltpu.VMEM((nch, nstate, cw), BF16),
            pltpu.VMEM((nch, tokens, cw), F32),
            pltpu.VMEM((tokens, 128), F32),
            pltpu.VMEM((kv_heads, channels, kw), BF16),
            pltpu.VMEM((kv_heads, tokens, kw), F32),
            pltpu.VMEM((kvh, nx, tokens, kw), BF16),
            pltpu.VMEM((kvh, nx, tokens, kw), BF16),
            pltpu.VMEM((kvh, nx, tokens, kw), BF16),
            pltpu.VMEM((kvh, nx, tokens, kw), BF16),
            pltpu.VMEM((nseq, kvh, tokens, kw), BF16),
            pltpu.VMEM((kvh, tokens * gs, att), BF16),
            pltpu.VMEM((kvh, tokens * gs, 2 * att), F32),
            dma((4,)),
            dma((3,)),
            dma((3,)),
            dma((nch,)),
            dma((nch,)),
            dma((kvh, nx)),
            dma((kvh, nx)),
            dma((kvh, nx, HALVES)),
            dma((kvh, nx, HALVES)),
            dma((nseq, kvh, HALVES)),
            dma((nseq, kvh, HALVES)),
        ],
        compiler_params=pltpu.CompilerParams(
            collective_id=0, has_side_effects=True, vmem_limit_bytes=62 * 1024 * 1024
        ),
        name="mixer_attention",
    )(
        x_in, b_in, c_in, dt_in.T, a_log.reshape(1, heads), conv_x, conv_bc, norm_gain.reshape(1, channels),
        z_in, w_kv.reshape(channels * kv_heads, kw), queries,
    )
    return pl.pallas_call(
        hand_out,
        out_shape=(
            jax.ShapeDtypeStruct((tokens, channels), BF16),
            jax.ShapeDtypeStruct((tokens, q_heads, att), BF16),
        ),
        in_specs=[hbm, hbm],
        out_specs=(hbm, hbm),
        scratch_shapes=[dma((2, OUT_PARTS))],
        compiler_params=pltpu.CompilerParams(vmem_limit_bytes=62 * 1024 * 1024),
        name="hand_out",
    )(mixed, attended)


def solution(mesh):
    return jax.shard_map(
        functools.partial(on_device, mesh.shape["seq"], mesh.shape["chan"]),
        mesh=mesh,
        in_specs=(
            P(("groups", "seq"), "chan"),
            P(("groups", "seq"), "chan", None),
            P(("groups", "seq"), "chan", None),
            P(("groups", "seq"), "chan"),
            P("chan"),
            P(("groups", "seq"), "chan"),
            P(None, "chan"),
            P(None, None, "chan", None),
            P("chan"),
            P("chan", None, None),
            P(("groups", "seq"), "chan", None),
        ),
        out_specs=(P(("groups", "seq"), "chan"), P(("groups", "seq"), "chan", None)),
        check_vma=False,
    )
```

```python
import functools
import math

import jax
import jax.numpy as jnp
from jax import lax
from jax.experimental import pallas as pl
from jax.experimental.pallas import tpu as pltpu
from jax.sharding import PartitionSpec as P

MESH = pl.DeviceIdType.MESH
F32 = jnp.float32
BF16 = jnp.bfloat16
RIM = 16
CORES = 2
WIDE = 256
ROWS = 512
HALVES = 2
OUT_PARTS = 4


def mm(a, b):
    return jnp.dot(a, b, preferred_element_type=F32)


def contract_rows(a, b):
    return lax.dot_general(a, b, (((0,), (0,)), ((), ())), preferred_element_type=F32)


def contract_lanes(a, b):
    return lax.dot_general(a, b, (((1,), (1,)), ((), ())), preferred_element_type=F32)


def silu(v):
    half = 0.5 * v
    return half + half * jnp.tanh(half)


def split2(v):
    high = v.astype(BF16)
    return high, (v - high.astype(F32)).astype(BF16)


def kernel(
    nseq, nchan, nstate, kv_heads,
    x_ref, b_ref, c_ref, dt_ref, alog_ref, tx_ref, tbc_ref, gain_ref, z_hbm, w_hbm, q_hbm,
    mix_out, att_ref,
    mix_ref, zv, wv, qv, rimx, rimb, rimc, xp, bcp, bcv, mask_cb, decay, xs, sl, sin, sout, ybuf, ssq,
    wp, kvp, s1, r1, s2, r2, kvall, qh, acc,
    in_sem, rim_send, rim_recv, st_send, st_recv,
    c1_send, c1_recv, c2_send, c2_recv, kv_send, kv_recv,
):
    tokens, channels = x_ref.shape
    heads = dt_ref.shape[0]
    head_width = channels // heads
    ngroups = b_ref.shape[1]
    gn = ngroups * nstate
    nch, _, cw = xs.shape
    per = nch // ngroups
    chg = channels // ngroups
    kvh = kv_heads // nchan
    att = qv.shape[2]
    gs = qv.shape[1] // kvh
    margin = tx_ref.shape[0] - 1
    base = 8 - margin
    nx = nchan // CORES
    me = lax.axis_index("seq")
    chan = lax.axis_index("chan")
    mx = chan // CORES
    core = chan % CORES
    mate = 1 - core
    mate_id = mx * CORES + mate

    def remote(src, dst, ss, rs, where):
        return pltpu.make_async_remote_copy(
            src_ref=src, dst_ref=dst, send_sem=ss, recv_sem=rs, device_id=where, device_id_type=MESH
        )

    z_copy = pltpu.make_async_copy(z_hbm, zv, in_sem.at[0])
    q_copy = pltpu.make_async_copy(q_hbm, qv, in_sem.at[1])
    w_copy = pltpu.make_async_copy(w_hbm, wv, in_sem.at[2])
    z_copy.start()
    q_copy.start()
    w_copy.start()

    barrier = pltpu.get_barrier_semaphore()

    @pl.when(me > 0)
    def _():
        pl.semaphore_signal(barrier, inc=1, device_id={"seq": me - 1}, device_id_type=MESH)

    @pl.when(me < nseq - 1)
    def _():
        pl.semaphore_signal(barrier, inc=1, device_id={"seq": me + 1}, device_id_type=MESH)

    pl.semaphore_signal(barrier, inc=1, device_id={"chan": mate_id}, device_id_type=MESH)
    for off in range(1, nx):
        other = ((mx + off) % nx) * CORES + core
        pl.semaphore_signal(barrier, inc=1, device_id={"chan": other}, device_id_type=MESH)
    pl.semaphore_wait(barrier, nx + jnp.minimum(me, 1) + jnp.minimum(nseq - 1 - me, 1))

    nxt = {"seq": jnp.minimum(me + 1, nseq - 1)}

    def rim_copies():
        return (
            remote(x_ref.at[pl.ds(tokens - RIM, RIM)], rimx, rim_send.at[0], rim_recv.at[0], nxt),
            remote(b_ref.at[pl.ds(tokens - RIM, RIM)], rimb, rim_send.at[1], rim_recv.at[1], nxt),
            remote(c_ref.at[pl.ds(tokens - RIM, RIM)], rimc, rim_send.at[2], rim_recv.at[2], nxt),
        )

    def state_copy(j):
        return remote(sout.at[j], sin.at[j], st_send.at[j], st_recv.at[j], nxt)

    def kv_copy(src, i, f):
        half = tokens // HALVES
        block = kvall.at[src, i, pl.ds(f * half, half)]
        return remote(block, block, kv_send.at[src, i, f], kv_recv.at[src, i, f], nxt)

    @pl.when(me < nseq - 1)
    def _():
        for copy in rim_copies():
            copy.start()

    @pl.when(me == 0)
    def _():
        rimx[...] = jnp.zeros_like(rimx)
        rimb[...] = jnp.zeros_like(rimb)
        rimc[...] = jnp.zeros_like(rimc)
        sin[...] = jnp.zeros_like(sin)

    step = jnp.log(1.0 + jnp.exp(dt_ref[...]))
    same = lax.broadcasted_iota(jnp.int32, (heads, heads), 0) == lax.broadcasted_iota(
        jnp.int32, (heads, heads), 1
    )
    rates = jnp.sum(jnp.where(same, jnp.exp(alog_ref[...]), 0.0), axis=1, keepdims=True)
    drop = -step * rates
    at_row = lax.broadcasted_iota(jnp.int32, (tokens, tokens), 0)
    at_col = lax.broadcasted_iota(jnp.int32, (tokens, tokens), 1)
    causal = at_row >= at_col
    lower = causal.astype(F32).astype(BF16)
    d1, rest = split2(drop)
    d2 = rest
    d3 = (drop - d1.astype(F32) - d2.astype(F32)).astype(BF16)
    running = contract_lanes(d1, lower) + contract_lanes(d2, lower) + contract_lanes(d3, lower)
    e_hi, e_lo = split2(jnp.exp(running))
    w_hi, w_lo = split2(jnp.exp(-running) * step)
    decay[0] = e_hi
    decay[1] = e_lo
    decay[2] = w_hi
    decay[3] = w_lo

    def spread(j):
        head = lax.broadcasted_iota(jnp.int32, (heads, cw), 0) * head_width
        lane = lax.broadcasted_iota(jnp.int32, (heads, cw), 1) + j * cw
        return ((lane >= head) & (lane < head + head_width)).astype(F32).astype(BF16)

    @pl.when(me > 0)
    def _():
        for copy in rim_copies():
            copy.wait_recv()

    for which, (ref, rim) in enumerate(((b_ref, rimb), (c_ref, rimc))):
        full = ref[...].astype(F32)
        ahead = rim[...].astype(F32)
        for g in range(ngroups):
            lanes = slice(which * gn + g * nstate, which * gn + (g + 1) * nstate)
            bcp[0:8, lanes] = ahead[8:16, g, :]
            bcp[8 : 8 + tokens, lanes] = full[:, g, :]
            summed = tbc_ref[which, 0, g : g + 1, :] * bcp[base : base + tokens, lanes]
            for k in range(1, margin + 1):
                taps = tbc_ref[which, k, g : g + 1, :]
                summed = summed + taps * bcp[base + k : base + k + tokens, lanes]
            bcv[:, lanes] = silu(summed).astype(BF16)
    for g in range(ngroups):
        cb = contract_lanes(
            bcv[:, gn + g * nstate : gn + (g + 1) * nstate], bcv[:, g * nstate : (g + 1) * nstate]
        )
        mask_cb[g] = jnp.where(causal, cb, 0.0).astype(BF16)

    pair = 2 if per % 2 == 0 else 1

    def conv_one(j, slot):
        lanes = pl.ds(pl.multiple_of(j * cw, cw), cw)
        g = j // per
        xp[slot, 0:8, :] = rimx[:, lanes].astype(F32)[8:16]
        xp[slot, 8 : 8 + tokens, :] = x_ref[:, lanes].astype(F32)
        total = tx_ref[0:1, lanes] * xp[slot, base : base + tokens, :]
        for k in range(1, margin + 1):
            total = total + tx_ref[k : k + 1, lanes] * xp[slot, base + k : base + k + tokens, :]
        conv = silu(total).astype(BF16).astype(F32)
        each = spread(j)
        scaled = (conv * (contract_rows(decay[2], each) + contract_rows(decay[3], each))).astype(BF16)
        xs[j] = scaled
        own = contract_rows(bcv[:, pl.ds(pl.multiple_of(g * nstate, nstate), nstate)], scaled)
        sl[j] = own * last_decay(j)

    pairs = nch // pair
    ahead_by = 2

    def take_states(p):
        for k in range(pair):
            j = p * pair + k
            state_copy(j).wait_recv()

            @pl.when(me < nseq - 1)
            def _(j=j):
                sout[j] = (sin[j].astype(F32) * last_decay(j) + sl[j]).astype(BF16)
                state_copy(j).start()

    def conv_chunks(p, c):
        for k in range(pair):
            conv_one(p * pair + k, k)

        @pl.when(me == 0)
        def _():
            for k in range(pair):
                j = p * pair + k
                sout[j] = sl[j].astype(BF16)
                state_copy(j).start()

        @pl.when((me == 1) & (p >= ahead_by))
        def _():
            take_states(p - ahead_by)

        return c

    def last_decay(j):
        each = spread(j)
        tail = slice(tokens - 128, tokens)
        got = contract_rows(decay[0, :, tail], each) + contract_rows(decay[1, :, tail], each)
        return got[127:128, :]

    lax.fori_loop(0, nch // pair, conv_chunks, 0)

    z_copy.wait()
    w_copy.wait()

    blk = WIDE // kv_heads
    prow = lax.broadcasted_iota(jnp.int32, (WIDE, WIDE), 0)
    pcol = lax.broadcasted_iota(jnp.int32, (WIDE, WIDE), 1)
    perm = (pcol == (prow % blk) * kv_heads + prow // blk).astype(F32).astype(BF16)
    w_parts = channels // blk // nch
    q_rows = tokens // nch

    def weights_part(j):
        for n in range(w_parts):
            at = j * w_parts + n
            moved = mm(perm, wv[pl.ds(pl.multiple_of(at * WIDE, WIDE), WIDE), :]).astype(BF16)
            for h in range(kv_heads):
                wp[h, pl.ds(pl.multiple_of(at * blk, blk), blk), :] = moved[h * blk : (h + 1) * blk]

    def query_part(j, c):
        qf = qv[pl.ds(j * q_rows, q_rows)].astype(F32)
        qn = qf * lax.rsqrt(jnp.mean(qf * qf, axis=-1, keepdims=True) + 1e-06)
        for i in range(kvh):
            qh[i, pl.ds(pl.multiple_of(j * q_rows * gs, q_rows * gs), q_rows * gs), :] = (
                qn[:, i * gs : (i + 1) * gs, :].reshape(q_rows * gs, att).astype(BF16)
            )

        return c

    def scan_chunks(p, c):
        @pl.when((me > 1) | ((me == 1) & (p >= pairs - ahead_by)))
        def _():
            take_states(p)

        sums = jnp.where((p * pair) % per == 0, 0.0, ssq[...])
        for k in range(pair):
            j = p * pair + k
            lanes = pl.ds(pl.multiple_of(j * cw, cw), cw)
            g = j // per
            weights_part(j)
            each = spread(j)
            gate = silu(zv[:, lanes].astype(F32)) * (
                contract_rows(decay[0], each) + contract_rows(decay[1], each)
            )
            c_rows = bcv[:, pl.ds(pl.multiple_of(gn + g * nstate, nstate), nstate)]
            y = (mm(mask_cb[g], xs[j]) + mm(c_rows, sin[j])) * gate
            ybuf[j] = y
            sq = y * y
            for m in range(cw // 128):
                sums = sums + sq[:, m * 128 : (m + 1) * 128]
        ssq[...] = sums
        return c

    def kv_dot(g, h):
        span = pl.ds(g * chg, chg)
        got = mm(mix_ref[:, span], wp[h, span, :])
        return got if g == 0 else kvp[h] + got

    ssq[...] = jnp.zeros_like(ssq)
    for g in range(ngroups):
        lax.fori_loop(g * per // pair, (g + 1) * per // pair, scan_chunks, 0)
        scale = lax.rsqrt(jnp.sum(ssq[...], axis=-1, keepdims=True) / chg + 1e-05)

        def norm_chunk(j, c):
            lanes = pl.ds(pl.multiple_of(j * cw, cw), cw)
            mix_ref[:, lanes] = (ybuf[j] * scale * gain_ref[0:1, lanes]).astype(BF16)
            return c

        lax.fori_loop(g * per, (g + 1) * per, norm_chunk, 0)
        if g < ngroups - 1:

            def kv_part(h, c):
                kvp[h] = kv_dot(g, h)
                return c

            lax.fori_loop(0, kv_heads, kv_part, 0)

    mix_copy = pltpu.make_async_copy(mix_ref, mix_out, in_sem.at[3])
    mix_copy.start()

    last = ngroups - 1

    def core_copy(i, cx):
        return remote(
            s1.at[i, cx], r1.at[i, cx], c1_send.at[i, cx], c1_recv.at[i, cx], {"chan": mate_id}
        )

    half = tokens // HALVES

    def chip_copy(i, to, slot, f):
        span = pl.ds(f * half, half)
        return remote(
            s2.at[i, to, span], r2.at[i, slot, span], c2_send.at[i, to, f], c2_recv.at[i, slot, f],
            {"chan": to * CORES + core},
        )

    for i in range(kvh):

        def to_mate(n, c, i=i):
            cx = (mx + 1 + n) % nx
            s1[i, cx] = kv_dot(last, (cx * CORES + mate) * kvh + i).astype(BF16)
            core_copy(i, cx).start()
            return c

        lax.fori_loop(0, nx, to_mate, 0)

        def to_chip(n, c, i=i):
            cx = (mx + 1 + n) % nx
            h = (cx * CORES + core) * kvh + i
            mine = kv_dot(last, h)
            core_copy(i, cx).wait_recv()
            both = mine + r1[i, cx].astype(F32)
            kvp[h] = both

            @pl.when(n < nx - 1)
            def _():
                s2[i, cx] = both.astype(BF16)
                for f in range(HALVES):
                    chip_copy(i, cx, mx, f).start()

            return c

        lax.fori_loop(0, nx, to_chip, 0)

    factor = att ** (-0.5) * math.log2(math.e)
    rows = min(ROWS, tokens * gs)
    parts = tokens * gs // rows

    def attend(i, src, own):
        for p in range(parts):
            span = slice(p * rows, (p + 1) * rows)
            seen = min(tokens, -(-(p + 1) * rows // (gs * 128)) * 128) if own else tokens
            keys = kvall[src, i, 0:seen, 0:att]
            values = jnp.concatenate([kvall[src, i, 0:seen, att:], jnp.ones((seen, att), BF16)], axis=1)
            weights = jnp.exp2(contract_lanes(qh[i, span, :], keys) * factor)
            if own:
                row = lax.broadcasted_iota(jnp.int32, (rows, seen), 0) + p * rows
                col = lax.broadcasted_iota(jnp.int32, (rows, seen), 1) * gs
                weights = jnp.where(row >= col, weights, 0.0)
            got = mm(weights.astype(BF16), values)
            acc[i, span, :] = got if own else acc[i, span, :] + got

    out_rows = tokens // nch

    def finish(i):
        def part(p, c):
            span = pl.ds(pl.multiple_of(p * out_rows * gs, out_rows * gs), out_rows * gs)
            done = acc[i, span, 0:att] / acc[i, span, att:]
            att_ref[pl.ds(p * out_rows, out_rows), i * gs : (i + 1) * gs, :] = done.astype(
                BF16
            ).reshape(out_rows, gs, att)
            return c

        lax.fori_loop(0, nch, part, 0)

    def earlier(back, c):
        src = me - back
        for i in range(kvh):
            for f in range(HALVES):
                kv_copy(src, i, f).wait_recv()

                @pl.when(me < nseq - 1)
                def _(i=i, f=f):
                    kv_copy(src, i, f).start()

            attend(i, src, False)

            @pl.when(back == me)
            def _(i=i):
                finish(i)

        return c

    q_copy.wait()
    lax.fori_loop(0, nch, query_part, 0)
    for i in range(kvh):
        for f in range(HALVES):
            span = slice(f * half, (f + 1) * half)
            total = kvp[chan * kvh + i, span]
            for off in range(1, nx):
                cx = (mx + off) % nx
                chip_copy(i, cx, cx, f).wait_recv()
                total = total + r2[i, cx, span].astype(F32)
            key = total[:, 0:att]
            key = key * lax.rsqrt(jnp.mean(key * key, axis=-1, keepdims=True) + 1e-06)
            kvall[me, i, span, 0:att] = key.astype(BF16)
            kvall[me, i, span, att:] = total[:, att:].astype(BF16)

            @pl.when(me < nseq - 1)
            def _(i=i, f=f):
                kv_copy(me, i, f).start()

        attend(i, me, True)

        @pl.when(me == 0)
        def _(i=i):
            finish(i)

    lax.fori_loop(1, me + 1, earlier, 0)

    mix_copy.wait()
    for i in range(kvh):
        for off in range(nx):
            core_copy(i, (mx + off) % nx).wait_send()
        for off in range(1, nx):
            for f in range(HALVES):
                chip_copy(i, (mx + off) % nx, mx, f).wait_send()

    @pl.when(me < nseq - 1)
    def _():
        for copy in rim_copies():
            copy.wait_send()
        for j in range(nch):
            state_copy(j).wait_send()

        def sent(s, c):
            for i in range(kvh):
                for f in range(HALVES):
                    kv_copy(s, i, f).wait_send()
            return c

        lax.fori_loop(0, me + 1, sent, 0)


def hand_out(a_in, b_in, a_out, b_out, a_mid, b_mid, sem_in, sem_out):
    rows = a_in.shape[0] // OUT_PARTS
    reads, writes = [], []
    for n in range(OUT_PARTS):
        span = pl.ds(n * rows, rows)
        for k, (src, mid, dst) in enumerate(((a_in, a_mid, a_out), (b_in, b_mid, b_out))):
            reads.append(pltpu.make_async_copy(src.at[span], mid.at[span], sem_in.at[k, n]))
            writes.append(pltpu.make_async_copy(mid.at[span], dst.at[span], sem_out.at[k, n]))
    for read in reads:
        read.start()
    for read, write in zip(reads, writes):
        read.wait()
        write.start()
    for write in writes:
        write.wait()


def on_device(nseq, nchan, x_in, b_in, c_in, dt_in, a_log, z_in, conv_x, conv_bc, norm_gain, w_kv, queries):
    tokens, channels = x_in.shape
    _, ngroups, nstate = b_in.shape
    gn = ngroups * nstate
    heads = dt_in.shape[1]
    kv_heads, kw = w_kv.shape[1:]
    q_heads, att = queries.shape[1:]
    kvh = kv_heads // nchan
    gs = q_heads // kvh
    cw = min(WIDE, channels // ngroups)
    nch = channels // cw
    nx = nchan // CORES
    vmem = pl.BlockSpec(memory_space=pltpu.VMEM)
    hbm = pl.BlockSpec(memory_space=pl.ANY)
    dma = pltpu.SemaphoreType.DMA
    mixed, attended = pl.pallas_call(
        functools.partial(kernel, nseq, nchan, nstate, kv_heads),
        out_shape=(
            jax.ShapeDtypeStruct((tokens, channels), BF16),
            jax.ShapeDtypeStruct((tokens, q_heads, att), BF16),
        ),
        in_specs=[vmem] * 8 + [hbm] * 3,
        out_specs=(hbm, vmem),
        scratch_shapes=[
            pltpu.VMEM((tokens, channels), BF16),
            pltpu.VMEM((tokens, channels), BF16),
            pltpu.VMEM((channels * kv_heads, kw), BF16),
            pltpu.VMEM((tokens, q_heads, att), BF16),
            pltpu.VMEM((RIM, channels), BF16),
            pltpu.VMEM((RIM, ngroups, nstate), BF16),
            pltpu.VMEM((RIM, ngroups, nstate), BF16),
            pltpu.VMEM((2, tokens + 8, cw), F32),
            pltpu.VMEM((tokens + 8, 2 * gn), F32),
            pltpu.VMEM((tokens, 2 * gn), BF16),
            pltpu.VMEM((ngroups, tokens, tokens), BF16),
            pltpu.VMEM((4, heads, tokens), BF16),
            pltpu.VMEM((nch, tokens, cw), BF16),
            pltpu.VMEM((nch, nstate, cw), F32),
            pltpu.VMEM((nch, nstate, cw), BF16),
            pltpu.VMEM((nch, nstate, cw), BF16),
            pltpu.VMEM((nch, tokens, cw), F32),
            pltpu.VMEM((tokens, 128), F32),
            pltpu.VMEM((kv_heads, channels, kw), BF16),
            pltpu.VMEM((kv_heads, tokens, kw), F32),
            pltpu.VMEM((kvh, nx, tokens, kw), BF16),
            pltpu.VMEM((kvh, nx, tokens, kw), BF16),
            pltpu.VMEM((kvh, nx, tokens, kw), BF16),
            pltpu.VMEM((kvh, nx, tokens, kw), BF16),
            pltpu.VMEM((nseq, kvh, tokens, kw), BF16),
            pltpu.VMEM((kvh, tokens * gs, att), BF16),
            pltpu.VMEM((kvh, tokens * gs, 2 * att), F32),
            dma((4,)),
            dma((3,)),
            dma((3,)),
            dma((nch,)),
            dma((nch,)),
            dma((kvh, nx)),
            dma((kvh, nx)),
            dma((kvh, nx, HALVES)),
            dma((kvh, nx, HALVES)),
            dma((nseq, kvh, HALVES)),
            dma((nseq, kvh, HALVES)),
        ],
        compiler_params=pltpu.CompilerParams(
            collective_id=0, has_side_effects=True, vmem_limit_bytes=62 * 1024 * 1024
        ),
        name="mixer_attention",
    )(
        x_in, b_in, c_in, dt_in.T, a_log.reshape(1, heads), conv_x, conv_bc, norm_gain.reshape(1, channels),
        z_in, w_kv.reshape(channels * kv_heads, kw), queries,
    )
    return pl.pallas_call(
        hand_out,
        out_shape=(
            jax.ShapeDtypeStruct((tokens, channels), BF16),
            jax.ShapeDtypeStruct((tokens, q_heads, att), BF16),
        ),
        in_specs=[hbm, hbm],
        out_specs=(hbm, hbm),
        scratch_shapes=[
            pltpu.VMEM((tokens, channels), BF16),
            pltpu.VMEM((tokens, q_heads, att), BF16),
            dma((2, OUT_PARTS)),
            dma((2, OUT_PARTS)),
        ],
        compiler_params=pltpu.CompilerParams(vmem_limit_bytes=62 * 1024 * 1024),
        name="hand_out",
    )(mixed, attended)


def solution(mesh):
    return jax.shard_map(
        functools.partial(on_device, mesh.shape["seq"], mesh.shape["chan"]),
        mesh=mesh,
        in_specs=(
            P(("groups", "seq"), "chan"),
            P(("groups", "seq"), "chan", None),
            P(("groups", "seq"), "chan", None),
            P(("groups", "seq"), "chan"),
            P("chan"),
            P(("groups", "seq"), "chan"),
            P(None, "chan"),
            P(None, None, "chan", None),
            P("chan"),
            P("chan", None, None),
            P(("groups", "seq"), "chan", None),
        ),
        out_specs=(P(("groups", "seq"), "chan"), P(("groups", "seq"), "chan", None)),
        check_vma=False,
    )
```

```python
import functools
import math

import jax
import jax.numpy as jnp
from jax import lax
from jax.experimental import pallas as pl
from jax.experimental.pallas import tpu as pltpu
from jax.sharding import PartitionSpec as P

MESH = pl.DeviceIdType.MESH
F32 = jnp.float32
BF16 = jnp.bfloat16
RIM = 16
CORES = 2
WIDE = 256
ROWS = 512
HALVES = 4
OUT_PARTS = 4


def mm(a, b):
    return jnp.dot(a, b, preferred_element_type=F32)


def contract_rows(a, b):
    return lax.dot_general(a, b, (((0,), (0,)), ((), ())), preferred_element_type=F32)


def contract_lanes(a, b):
    return lax.dot_general(a, b, (((1,), (1,)), ((), ())), preferred_element_type=F32)


def silu(v):
    half = 0.5 * v
    return half + half * jnp.tanh(half)


def split2(v):
    high = v.astype(BF16)
    return high, (v - high.astype(F32)).astype(BF16)


def kernel(
    nseq, nchan, nstate, kv_heads,
    x_ref, b_ref, c_ref, dt_ref, alog_ref, tx_ref, tbc_ref, gain_ref, z_hbm, w_hbm, q_hbm,
    mix_out, att_ref,
    mix_ref, zv, wv, qv, rimx, rimb, rimc, xp, bcp, bcv, mask_cb, decay, xs, sl, sin, sout, ybuf, ssq,
    wp, kvp, s1, r1, s2, r2, kvall, qh, acc,
    in_sem, rim_send, rim_recv, st_send, st_recv,
    c1_send, c1_recv, c2_send, c2_recv, kv_send, kv_recv,
):
    tokens, channels = x_ref.shape
    heads = dt_ref.shape[0]
    head_width = channels // heads
    ngroups = b_ref.shape[1]
    gn = ngroups * nstate
    nch, _, cw = xs.shape
    per = nch // ngroups
    chg = channels // ngroups
    kvh = kv_heads // nchan
    att = qv.shape[2]
    gs = qv.shape[1] // kvh
    margin = tx_ref.shape[0] - 1
    base = 8 - margin
    nx = nchan // CORES
    me = lax.axis_index("seq")
    chan = lax.axis_index("chan")
    mx = chan // CORES
    core = chan % CORES
    mate = 1 - core
    mate_id = mx * CORES + mate

    def remote(src, dst, ss, rs, where):
        return pltpu.make_async_remote_copy(
            src_ref=src, dst_ref=dst, send_sem=ss, recv_sem=rs, device_id=where, device_id_type=MESH
        )

    z_copy = pltpu.make_async_copy(z_hbm, zv, in_sem.at[0])
    q_copy = pltpu.make_async_copy(q_hbm, qv, in_sem.at[1])
    w_copy = pltpu.make_async_copy(w_hbm, wv, in_sem.at[2])
    z_copy.start()
    q_copy.start()
    w_copy.start()

    barrier = pltpu.get_barrier_semaphore()

    @pl.when(me > 0)
    def _():
        pl.semaphore_signal(barrier, inc=1, device_id={"seq": me - 1}, device_id_type=MESH)

    @pl.when(me < nseq - 1)
    def _():
        pl.semaphore_signal(barrier, inc=1, device_id={"seq": me + 1}, device_id_type=MESH)

    pl.semaphore_signal(barrier, inc=1, device_id={"chan": mate_id}, device_id_type=MESH)
    for off in range(1, nx):
        other = ((mx + off) % nx) * CORES + core
        pl.semaphore_signal(barrier, inc=1, device_id={"chan": other}, device_id_type=MESH)
    pl.semaphore_wait(barrier, nx + jnp.minimum(me, 1) + jnp.minimum(nseq - 1 - me, 1))

    nxt = {"seq": jnp.minimum(me + 1, nseq - 1)}

    def rim_copies():
        return (
            remote(x_ref.at[pl.ds(tokens - RIM, RIM)], rimx, rim_send.at[0], rim_recv.at[0], nxt),
            remote(b_ref.at[pl.ds(tokens - RIM, RIM)], rimb, rim_send.at[1], rim_recv.at[1], nxt),
            remote(c_ref.at[pl.ds(tokens - RIM, RIM)], rimc, rim_send.at[2], rim_recv.at[2], nxt),
        )

    def state_copy(j):
        return remote(sout.at[j], sin.at[j], st_send.at[j], st_recv.at[j], nxt)

    def kv_copy(src, i, f):
        half = tokens // HALVES
        block = kvall.at[src, i, pl.ds(f * half, half)]
        return remote(block, block, kv_send.at[src, i, f], kv_recv.at[src, i, f], nxt)

    @pl.when(me < nseq - 1)
    def _():
        for copy in rim_copies():
            copy.start()

    @pl.when(me == 0)
    def _():
        rimx[...] = jnp.zeros_like(rimx)
        rimb[...] = jnp.zeros_like(rimb)
        rimc[...] = jnp.zeros_like(rimc)
        sin[...] = jnp.zeros_like(sin)

    step = jnp.log(1.0 + jnp.exp(dt_ref[...]))
    same = lax.broadcasted_iota(jnp.int32, (heads, heads), 0) == lax.broadcasted_iota(
        jnp.int32, (heads, heads), 1
    )
    rates = jnp.sum(jnp.where(same, jnp.exp(alog_ref[...]), 0.0), axis=1, keepdims=True)
    drop = -step * rates
    at_row = lax.broadcasted_iota(jnp.int32, (tokens, tokens), 0)
    at_col = lax.broadcasted_iota(jnp.int32, (tokens, tokens), 1)
    causal = at_row >= at_col
    lower = causal.astype(F32).astype(BF16)
    d1, rest = split2(drop)
    d2 = rest
    d3 = (drop - d1.astype(F32) - d2.astype(F32)).astype(BF16)
    running = contract_lanes(d1, lower) + contract_lanes(d2, lower) + contract_lanes(d3, lower)
    e_hi, e_lo = split2(jnp.exp(running))
    w_hi, w_lo = split2(jnp.exp(-running) * step)
    decay[0] = e_hi
    decay[1] = e_lo
    decay[2] = w_hi
    decay[3] = w_lo

    def spread(j):
        head = lax.broadcasted_iota(jnp.int32, (heads, cw), 0) * head_width
        lane = lax.broadcasted_iota(jnp.int32, (heads, cw), 1) + j * cw
        return ((lane >= head) & (lane < head + head_width)).astype(F32).astype(BF16)

    @pl.when(me > 0)
    def _():
        for copy in rim_copies():
            copy.wait_recv()

    def conv_bc(which, ref, rim):
        full = ref[...].astype(F32)
        ahead = rim[...].astype(F32)
        for g in range(ngroups):
            lanes = slice(which * gn + g * nstate, which * gn + (g + 1) * nstate)
            bcp[0:8, lanes] = ahead[8:16, g, :]
            bcp[8 : 8 + tokens, lanes] = full[:, g, :]
            summed = tbc_ref[which, 0, g : g + 1, :] * bcp[base : base + tokens, lanes]
            for k in range(1, margin + 1):
                taps = tbc_ref[which, k, g : g + 1, :]
                summed = summed + taps * bcp[base + k : base + k + tokens, lanes]
            bcv[:, lanes] = silu(summed).astype(BF16)

    conv_bc(0, b_ref, rimb)

    pair = 2 if per % 2 == 0 else 1

    def conv_one(j, slot):
        lanes = pl.ds(pl.multiple_of(j * cw, cw), cw)
        g = j // per
        xp[slot, 0:8, :] = rimx[:, lanes].astype(F32)[8:16]
        xp[slot, 8 : 8 + tokens, :] = x_ref[:, lanes].astype(F32)
        total = tx_ref[0:1, lanes] * xp[slot, base : base + tokens, :]
        for k in range(1, margin + 1):
            total = total + tx_ref[k : k + 1, lanes] * xp[slot, base + k : base + k + tokens, :]
        conv = silu(total).astype(BF16).astype(F32)
        each = spread(j)
        scaled = (conv * (contract_rows(decay[2], each) + contract_rows(decay[3], each))).astype(BF16)
        xs[j] = scaled
        own = contract_rows(bcv[:, pl.ds(pl.multiple_of(g * nstate, nstate), nstate)], scaled)
        sl[j] = own * last_decay(j)

    pairs = nch // pair
    ahead_by = 2

    def take_states(p):
        for k in range(pair):
            j = p * pair + k
            state_copy(j).wait_recv()

            @pl.when(me < nseq - 1)
            def _(j=j):
                sout[j] = (sin[j].astype(F32) * last_decay(j) + sl[j]).astype(BF16)
                state_copy(j).start()

    def conv_chunks(p, c):
        for k in range(pair):
            conv_one(p * pair + k, k)

        @pl.when(me == 0)
        def _():
            for k in range(pair):
                j = p * pair + k
                sout[j] = sl[j].astype(BF16)
                state_copy(j).start()

        @pl.when((me == 1) & (p >= ahead_by))
        def _():
            take_states(p - ahead_by)

        return c

    def last_decay(j):
        each = spread(j)
        tail = slice(tokens - 128, tokens)
        got = contract_rows(decay[0, :, tail], each) + contract_rows(decay[1, :, tail], each)
        return got[127:128, :]

    lax.fori_loop(0, nch // pair, conv_chunks, 0)

    conv_bc(1, c_ref, rimc)
    for g in range(ngroups):
        cb = contract_lanes(
            bcv[:, gn + g * nstate : gn + (g + 1) * nstate], bcv[:, g * nstate : (g + 1) * nstate]
        )
        mask_cb[g] = jnp.where(causal, cb, 0.0).astype(BF16)

    z_copy.wait()
    w_copy.wait()

    blk = WIDE // kv_heads
    prow = lax.broadcasted_iota(jnp.int32, (WIDE, WIDE), 0)
    pcol = lax.broadcasted_iota(jnp.int32, (WIDE, WIDE), 1)
    perm = (pcol == (prow % blk) * kv_heads + prow // blk).astype(F32).astype(BF16)
    w_parts = channels // blk // nch
    q_rows = tokens // nch

    def weights_part(j):
        for n in range(w_parts):
            at = j * w_parts + n
            moved = mm(perm, wv[pl.ds(pl.multiple_of(at * WIDE, WIDE), WIDE), :]).astype(BF16)
            for h in range(kv_heads):
                wp[h, pl.ds(pl.multiple_of(at * blk, blk), blk), :] = moved[h * blk : (h + 1) * blk]

    def query_part(j, c):
        qf = qv[pl.ds(j * q_rows, q_rows)].astype(F32)
        qn = qf * lax.rsqrt(jnp.mean(qf * qf, axis=-1, keepdims=True) + 1e-06)
        for i in range(kvh):
            qh[i, pl.ds(pl.multiple_of(j * q_rows * gs, q_rows * gs), q_rows * gs), :] = (
                qn[:, i * gs : (i + 1) * gs, :].reshape(q_rows * gs, att).astype(BF16)
            )

        return c

    def scan_chunks(p, c):
        @pl.when((me > 1) | ((me == 1) & (p >= pairs - ahead_by)))
        def _():
            take_states(p)

        sums = jnp.where((p * pair) % per == 0, 0.0, ssq[...])
        for k in range(pair):
            j = p * pair + k
            lanes = pl.ds(pl.multiple_of(j * cw, cw), cw)
            g = j // per
            weights_part(j)
            each = spread(j)
            gate = silu(zv[:, lanes].astype(F32)) * (
                contract_rows(decay[0], each) + contract_rows(decay[1], each)
            )
            c_rows = bcv[:, pl.ds(pl.multiple_of(gn + g * nstate, nstate), nstate)]
            y = (mm(mask_cb[g], xs[j]) + mm(c_rows, sin[j])) * gate
            ybuf[j] = y
            sq = y * y
            for m in range(cw // 128):
                sums = sums + sq[:, m * 128 : (m + 1) * 128]
        ssq[...] = sums
        return c

    def kv_dot(g, h):
        span = pl.ds(g * chg, chg)
        got = mm(mix_ref[:, span], wp[h, span, :])
        return got if g == 0 else kvp[h] + got

    ssq[...] = jnp.zeros_like(ssq)
    for g in range(ngroups):
        lax.fori_loop(g * per // pair, (g + 1) * per // pair, scan_chunks, 0)
        scale = lax.rsqrt(jnp.sum(ssq[...], axis=-1, keepdims=True) / chg + 1e-05)

        def norm_chunk(j, c):
            lanes = pl.ds(pl.multiple_of(j * cw, cw), cw)
            mix_ref[:, lanes] = (ybuf[j] * scale * gain_ref[0:1, lanes]).astype(BF16)
            return c

        lax.fori_loop(g * per, (g + 1) * per, norm_chunk, 0)
        if g < ngroups - 1:

            def kv_part(h, c):
                kvp[h] = kv_dot(g, h)
                return c

            lax.fori_loop(0, kv_heads, kv_part, 0)

    mix_copy = pltpu.make_async_copy(mix_ref, mix_out, in_sem.at[3])
    mix_copy.start()

    last = ngroups - 1

    def core_copy(i, cx):
        return remote(
            s1.at[i, cx], r1.at[i, cx], c1_send.at[i, cx], c1_recv.at[i, cx], {"chan": mate_id}
        )

    half = tokens // HALVES

    def chip_copy(i, to, slot, f):
        span = pl.ds(f * half, half)
        return remote(
            s2.at[i, to, span], r2.at[i, slot, span], c2_send.at[i, to, f], c2_recv.at[i, slot, f],
            {"chan": to * CORES + core},
        )

    for i in range(kvh):

        def to_mate(n, c, i=i):
            cx = (mx + 1 + n) % nx
            s1[i, cx] = kv_dot(last, (cx * CORES + mate) * kvh + i).astype(BF16)
            core_copy(i, cx).start()
            return c

        lax.fori_loop(0, nx, to_mate, 0)

        def to_chip(n, c, i=i):
            cx = (mx + 1 + n) % nx
            h = (cx * CORES + core) * kvh + i
            mine = kv_dot(last, h)
            core_copy(i, cx).wait_recv()
            both = mine + r1[i, cx].astype(F32)
            kvp[h] = both

            @pl.when(n < nx - 1)
            def _():
                s2[i, cx] = both.astype(BF16)
                for f in range(HALVES):
                    chip_copy(i, cx, mx, f).start()

            return c

        lax.fori_loop(0, nx, to_chip, 0)

    factor = att ** (-0.5) * math.log2(math.e)
    rows = min(ROWS, tokens * gs)
    parts = tokens * gs // rows

    def attend(i, src, own):
        for p in range(parts):
            span = slice(p * rows, (p + 1) * rows)
            seen = min(tokens, -(-(p + 1) * rows // (gs * 128)) * 128) if own else tokens
            keys = kvall[src, i, 0:seen, 0:att]
            values = jnp.concatenate([kvall[src, i, 0:seen, att:], jnp.ones((seen, att), BF16)], axis=1)
            weights = jnp.exp2(contract_lanes(qh[i, span, :], keys) * factor)
            if own:
                row = lax.broadcasted_iota(jnp.int32, (rows, seen), 0) + p * rows
                col = lax.broadcasted_iota(jnp.int32, (rows, seen), 1) * gs
                weights = jnp.where(row >= col, weights, 0.0)
            got = mm(weights.astype(BF16), values)
            acc[i, span, :] = got if own else acc[i, span, :] + got

    out_rows = tokens // nch

    def finish(i):
        def part(p, c):
            span = pl.ds(pl.multiple_of(p * out_rows * gs, out_rows * gs), out_rows * gs)
            done = acc[i, span, 0:att] / acc[i, span, att:]
            att_ref[pl.ds(p * out_rows, out_rows), i * gs : (i + 1) * gs, :] = done.astype(
                BF16
            ).reshape(out_rows, gs, att)
            return c

        lax.fori_loop(0, nch, part, 0)

    def earlier(back, c):
        src = me - back
        for i in range(kvh):
            for f in range(HALVES):
                kv_copy(src, i, f).wait_recv()

                @pl.when(me < nseq - 1)
                def _(i=i, f=f):
                    kv_copy(src, i, f).start()

            attend(i, src, False)

            @pl.when(back == me)
            def _(i=i):
                finish(i)

        return c

    for i in range(kvh):
        for f in range(HALVES):
            span = slice(f * half, (f + 1) * half)
            total = kvp[chan * kvh + i, span]
            for off in range(1, nx):
                cx = (mx + off) % nx
                chip_copy(i, cx, cx, f).wait_recv()
                total = total + r2[i, cx, span].astype(F32)
            key = total[:, 0:att]
            key = key * lax.rsqrt(jnp.mean(key * key, axis=-1, keepdims=True) + 1e-06)
            kvall[me, i, span, 0:att] = key.astype(BF16)
            kvall[me, i, span, att:] = total[:, att:].astype(BF16)

            @pl.when(me < nseq - 1)
            def _(i=i, f=f):
                kv_copy(me, i, f).start()

        if i == 0:
            q_copy.wait()
            lax.fori_loop(0, nch, query_part, 0)
        attend(i, me, True)

        @pl.when(me == 0)
        def _(i=i):
            finish(i)

    lax.fori_loop(1, me + 1, earlier, 0)

    mix_copy.wait()
    for i in range(kvh):
        for off in range(nx):
            core_copy(i, (mx + off) % nx).wait_send()
        for off in range(1, nx):
            for f in range(HALVES):
                chip_copy(i, (mx + off) % nx, mx, f).wait_send()

    @pl.when(me < nseq - 1)
    def _():
        for copy in rim_copies():
            copy.wait_send()
        for j in range(nch):
            state_copy(j).wait_send()

        def sent(s, c):
            for i in range(kvh):
                for f in range(HALVES):
                    kv_copy(s, i, f).wait_send()
            return c

        lax.fori_loop(0, me + 1, sent, 0)


def hand_out(a_in, b_in, a_out, b_out, a_mid, b_mid, sem_in, sem_out):
    rows = a_in.shape[0] // OUT_PARTS
    reads, writes = [], []
    for n in range(OUT_PARTS):
        span = pl.ds(n * rows, rows)
        for k, (src, mid, dst) in enumerate(((a_in, a_mid, a_out), (b_in, b_mid, b_out))):
            reads.append(pltpu.make_async_copy(src.at[span], mid.at[span], sem_in.at[k, n]))
            writes.append(pltpu.make_async_copy(mid.at[span], dst.at[span], sem_out.at[k, n]))
    for read in reads:
        read.start()
    for read, write in zip(reads, writes):
        read.wait()
        write.start()
    for write in writes:
        write.wait()


def on_device(nseq, nchan, x_in, b_in, c_in, dt_in, a_log, z_in, conv_x, conv_bc, norm_gain, w_kv, queries):
    tokens, channels = x_in.shape
    _, ngroups, nstate = b_in.shape
    gn = ngroups * nstate
    heads = dt_in.shape[1]
    kv_heads, kw = w_kv.shape[1:]
    q_heads, att = queries.shape[1:]
    kvh = kv_heads // nchan
    gs = q_heads // kvh
    cw = min(WIDE, channels // ngroups)
    nch = channels // cw
    nx = nchan // CORES
    vmem = pl.BlockSpec(memory_space=pltpu.VMEM)
    hbm = pl.BlockSpec(memory_space=pl.ANY)
    dma = pltpu.SemaphoreType.DMA
    mixed, attended = pl.pallas_call(
        functools.partial(kernel, nseq, nchan, nstate, kv_heads),
        out_shape=(
            jax.ShapeDtypeStruct((tokens, channels), BF16),
            jax.ShapeDtypeStruct((tokens, q_heads, att), BF16),
        ),
        in_specs=[vmem] * 8 + [hbm] * 3,
        out_specs=(hbm, vmem),
        scratch_shapes=[
            pltpu.VMEM((tokens, channels), BF16),
            pltpu.VMEM((tokens, channels), BF16),
            pltpu.VMEM((channels * kv_heads, kw), BF16),
            pltpu.VMEM((tokens, q_heads, att), BF16),
            pltpu.VMEM((RIM, channels), BF16),
            pltpu.VMEM((RIM, ngroups, nstate), BF16),
            pltpu.VMEM((RIM, ngroups, nstate), BF16),
            pltpu.VMEM((2, tokens + 8, cw), F32),
            pltpu.VMEM((tokens + 8, 2 * gn), F32),
            pltpu.VMEM((tokens, 2 * gn), BF16),
            pltpu.VMEM((ngroups, tokens, tokens), BF16),
            pltpu.VMEM((4, heads, tokens), BF16),
            pltpu.VMEM((nch, tokens, cw), BF16),
            pltpu.VMEM((nch, nstate, cw), F32),
            pltpu.VMEM((nch, nstate, cw), BF16),
            pltpu.VMEM((nch, nstate, cw), BF16),
            pltpu.VMEM((nch, tokens, cw), F32),
            pltpu.VMEM((tokens, 128), F32),
            pltpu.VMEM((kv_heads, channels, kw), BF16),
            pltpu.VMEM((kv_heads, tokens, kw), F32),
            pltpu.VMEM((kvh, nx, tokens, kw), BF16),
            pltpu.VMEM((kvh, nx, tokens, kw), BF16),
            pltpu.VMEM((kvh, nx, tokens, kw), BF16),
            pltpu.VMEM((kvh, nx, tokens, kw), BF16),
            pltpu.VMEM((nseq, kvh, tokens, kw), BF16),
            pltpu.VMEM((kvh, tokens * gs, att), BF16),
            pltpu.VMEM((kvh, tokens * gs, 2 * att), F32),
            dma((4,)),
            dma((3,)),
            dma((3,)),
            dma((nch,)),
            dma((nch,)),
            dma((kvh, nx)),
            dma((kvh, nx)),
            dma((kvh, nx, HALVES)),
            dma((kvh, nx, HALVES)),
            dma((nseq, kvh, HALVES)),
            dma((nseq, kvh, HALVES)),
        ],
        compiler_params=pltpu.CompilerParams(
            collective_id=0, has_side_effects=True, vmem_limit_bytes=62 * 1024 * 1024
        ),
        name="mixer_attention",
    )(
        x_in, b_in, c_in, dt_in.T, a_log.reshape(1, heads), conv_x, conv_bc, norm_gain.reshape(1, channels),
        z_in, w_kv.reshape(channels * kv_heads, kw), queries,
    )
    return pl.pallas_call(
        hand_out,
        out_shape=(
            jax.ShapeDtypeStruct((tokens, channels), BF16),
            jax.ShapeDtypeStruct((tokens, q_heads, att), BF16),
        ),
        in_specs=[hbm, hbm],
        out_specs=(hbm, hbm),
        scratch_shapes=[
            pltpu.VMEM((tokens, channels), BF16),
            pltpu.VMEM((tokens, q_heads, att), BF16),
            dma((2, OUT_PARTS)),
            dma((2, OUT_PARTS)),
        ],
        compiler_params=pltpu.CompilerParams(vmem_limit_bytes=62 * 1024 * 1024),
        name="hand_out",
    )(mixed, attended)


def solution(mesh):
    return jax.shard_map(
        functools.partial(on_device, mesh.shape["seq"], mesh.shape["chan"]),
        mesh=mesh,
        in_specs=(
            P(("groups", "seq"), "chan"),
            P(("groups", "seq"), "chan", None),
            P(("groups", "seq"), "chan", None),
            P(("groups", "seq"), "chan"),
            P("chan"),
            P(("groups", "seq"), "chan"),
            P(None, "chan"),
            P(None, None, "chan", None),
            P("chan"),
            P("chan", None, None),
            P(("groups", "seq"), "chan", None),
        ),
        out_specs=(P(("groups", "seq"), "chan"), P(("groups", "seq"), "chan", None)),
        check_vma=False,
    )
```
